32 devices in a mesh: img: 8 (over z, x), txt: 4 (over y, core).
Axes of the slice: x: 2, y: 2, z: 4, core: 2. Of those that a mesh axis runs over, the one named last changes fastest.
Arguments:
- image_tokens: bfloat16 [4096, 256], P(('img', 'txt')), may hold values from -6 to 6
- prompt_tokens: bfloat16 [768, 256], P(('txt', 'img')), may hold values from -6 to 6
- category_ids: int32 [768], P(('txt', 'img')), may hold values from 0 to 47, as said below
- prompt_valid: int32 [768], P(('txt', 'img')), may hold values from 0 to 1, as said below
- image_gain: float32 [256], replicated, may hold values from 0.5 to 1.5
- prompt_gain: float32 [256], replicated, may hold values from 0.5 to 1.5
- query_weight: bfloat16 [256, 1024], replicated, may hold values from -1.7 to 1.7
- key_weight: bfloat16 [256, 1024], replicated, may hold values from -1.7 to 1.7
- image_value_weight: bfloat16 [256, 1024], replicated, may hold values from -0.375 to 0.375
- prompt_value_weight: bfloat16 [256, 1024], replicated, may hold values from -0.375 to 0.375
- image_out_weight: bfloat16 [1024, 256], replicated, may hold values from -0.1875 to 0.1875
- prompt_out_weight: bfloat16 [1024, 256], replicated, may hold values from -0.1875 to 0.1875
- image_layer_scale: float32 [256], replicated, may hold values from 1 to 4
- prompt_layer_scale: float32 [256], replicated, may hold values from 1 to 4
Outputs:
- joined_image: bfloat16 [4096, 256], P(('img', 'txt'))
- joined_prompt: bfloat16 [768, 256], P(('txt', 'img'))
- category_embed: float32 [48, 256], replicated
The draws below stay inside these ranges and needn't reach their ends.
Inputs may be any that keep to these rules, and one draw needn't show every extreme that they name: `category_ids`: along the prompt the ids never fall; each of the 48 categories holds between 4 and 28 consecutive tokens. `prompt_valid`: within each category the tokens marked 1 come first, and at least one token is marked 1.
All inputs are finite; a program needn't handle non-finite values.
Results may differ from the reference program's by a relative error of at most 0.009.
The reference program's roundings to bfloat16 on the way count: a program that leaves them out, or rounds other values in their place, can miss the bound.
Values may be sent and summed in bfloat16 or wider, within the bound.
A program may use at most 128 MiB of HBM per device.

```python
import math
import jax
import jax.numpy as jnp
from jax import lax

D = 256
HEADS = 4
HD = 256
NI = 4096
NT = 768
IMG_BLK = 512
TXT_BLK = 192
CATS = 48
N_IMG = 8
N_TXT = 4


def category_starts(key):
    jitter = jax.random.randint(jax.random.fold_in(key, 11), (CATS - 1,), -6, 7)
    return jnp.arange(1, CATS, dtype=jnp.int32) * 16 + jitter.astype(jnp.int32)


def category_of(starts):
    positions = jnp.arange(NT, dtype=jnp.int32)
    return jnp.sum((positions[:, None] >= starts[None, :]).astype(jnp.int32), axis=1).astype(jnp.int32)


def draw_category_ids(key, part):
    return category_of(category_starts(key))


def draw_prompt_valid(key, part):
    starts = category_starts(key)
    lower = jnp.concatenate([jnp.zeros((1,), jnp.int32), starts])
    upper = jnp.concatenate([starts, jnp.full((1,), NT, jnp.int32)])
    kept = jax.random.randint(jax.random.fold_in(key, 23), (CATS,), 1, upper - lower + 1)
    owner = category_of(starts)
    offset = jnp.arange(NT, dtype=jnp.int32) - lower[owner]
    return (offset < kept[owner]).astype(jnp.int32)


def score_weight(key, salt):
    spread = 1.25 / math.sqrt(D)
    base = jnp.clip(jax.random.normal(jax.random.fold_in(key, salt), (D, HEADS * HD), jnp.float32), -6.0, 6.0) * spread
    return base.astype(jnp.bfloat16)


def draw_query_weight(key, part):
    return score_weight(key, 51)


def draw_key_weight(key, part):
    return score_weight(key, 52)


def shard_levels(rng, shape, split, low, largest):
    level, own = 1.0, jax.random.fold_in(rng, 6)
    for position, blocks in split:
        steps = jnp.exp(jax.random.uniform(jax.random.fold_in(own, position), (blocks,), jnp.float32, low / len(split), largest / len(split)))
        level = level * jnp.repeat(steps, shape[position] // blocks).reshape([-1 if axis == position else 1 for axis in range(len(shape))])
    return level


def gaussian(own_key, extent, deviation, reach, pieces=(), kind=jnp.bfloat16):
    entries = jax.random.normal(own_key, extent, jnp.float32) * deviation
    if len(pieces) > 0:
        entries = shard_levels(own_key, extent, pieces, -0.22, 0.18) * entries
    return jnp.clip(entries, min=-reach, max=reach).astype(kind)


def setup_inputs(seed: int = 0) -> dict:
    arg_keys = jax.random.split(jax.random.key(seed), 15)
    return {
        "image_tokens": gaussian(arg_keys[0], (NI, D), 1.0, 6.0, ((0, 32),)),
        "prompt_tokens": gaussian(arg_keys[1], (NT, D), 1.0, 6.0, ((0, 32),)),
        "category_ids": draw_category_ids(jax.random.fold_in(arg_keys[14], 71), 0),
        "prompt_valid": draw_prompt_valid(jax.random.fold_in(arg_keys[14], 71), 0),
        "image_gain": jnp.clip(1.0 + 0.1 * jax.random.normal(arg_keys[4], (D,), jnp.float32), 0.5, 1.5),
        "prompt_gain": jnp.clip(1.0 + 0.1 * jax.random.normal(arg_keys[5], (D,), jnp.float32), 0.5, 1.5),
        "query_weight": draw_query_weight(jax.random.fold_in(arg_keys[14], 71), 0),
        "key_weight": draw_key_weight(jax.random.fold_in(arg_keys[14], 71), 0),
        "image_value_weight": gaussian(arg_keys[8], (D, HEADS * HD), D ** -0.5, 0.375),
        "prompt_value_weight": gaussian(arg_keys[9], (D, HEADS * HD), D ** -0.5, 0.375),
        "image_out_weight": gaussian(arg_keys[10], (HEADS * HD, D), (HEADS * HD) ** -0.5, 0.1875),
        "prompt_out_weight": gaussian(arg_keys[11], (HEADS * HD, D), (HEADS * HD) ** -0.5, 0.1875),
        "image_layer_scale": jnp.clip(jnp.exp(jax.random.uniform(arg_keys[12], (D,), jnp.float32, math.log(1.0), math.log(4.0))), 1.0, 4.0),
        "prompt_layer_scale": jnp.clip(jnp.exp(jax.random.uniform(arg_keys[13], (D,), jnp.float32, math.log(1.0), math.log(4.0))), 1.0, 4.0),
    }


EPSILON = 1e-05
MASKED = -1e+30

def normalize(tokens_in, gain_row):
    values = tokens_in.astype(jnp.float32)
    average = lax.optimization_barrier(jnp.mean(values, axis=-1, keepdims=True))
    centered = values - average
    variance = lax.optimization_barrier(jnp.mean(centered * centered, axis=-1, keepdims=True))
    return (centered * lax.rsqrt(variance + EPSILON) * gain_row).astype(jnp.bfloat16)

def reference(image_tokens, prompt_tokens, category_ids, prompt_valid, image_gain, prompt_gain, query_weight, key_weight, image_value_weight, prompt_value_weight, image_out_weight, prompt_out_weight, image_layer_scale, prompt_layer_scale):
    embed_width = query_weight.shape[1]
    head_count = embed_width // HD
    image_normed = normalize(image_tokens, image_gain)
    prompt_normed = normalize(prompt_tokens, prompt_gain)
    queries = jnp.dot(image_normed.astype(jnp.float32), query_weight.astype(jnp.float32), preferred_element_type=jnp.float32).astype(jnp.bfloat16)
    image_values = jnp.dot(image_normed.astype(jnp.float32), image_value_weight.astype(jnp.float32), preferred_element_type=jnp.float32).astype(jnp.bfloat16)
    prompt_keys = jnp.dot(prompt_normed.astype(jnp.float32), key_weight.astype(jnp.float32), preferred_element_type=jnp.float32).astype(jnp.bfloat16)
    prompt_values = jnp.dot(prompt_normed.astype(jnp.float32), prompt_value_weight.astype(jnp.float32), preferred_element_type=jnp.float32).astype(jnp.bfloat16)
    key_heads = prompt_keys.reshape(NT, head_count, HD).astype(jnp.float32)
    value_blocks = prompt_values.reshape(N_TXT, TXT_BLK, head_count, HD).astype(jnp.float32)
    query_blocks = queries.reshape(N_IMG, IMG_BLK, head_count, HD)
    image_value_blocks = image_values.reshape(N_IMG, IMG_BLK, head_count, HD)
    is_valid = (prompt_valid > 0)[None, None, :]
    image_out = image_out_weight.astype(jnp.float32)

    def block_scores(query_block):
        return jnp.einsum('ihd,thd->hit', query_block.astype(jnp.float32), key_heads) / math.sqrt(HD)

    def first_pass(carry, query_block):
        col_top, col_sum = carry
        scores = block_scores(query_block)
        masked = jnp.where(is_valid, scores, MASKED)
        row_top = lax.optimization_barrier(jnp.max(masked, axis=2))
        row_exp = jnp.where(is_valid, jnp.exp(masked - row_top[:, :, None]), 0.0)
        row_sum = lax.optimization_barrier(jnp.sum(row_exp, axis=2))
        rounded = lax.optimization_barrier(row_exp.astype(jnp.bfloat16)).astype(jnp.float32)
        split_weights = rounded.reshape(head_count, IMG_BLK, N_TXT, TXT_BLK)
        image_parts = jnp.einsum('hibt,bthd->bihd', split_weights, value_blocks) / row_sum.T[None, :, :, None]
        image_parts = image_parts.reshape(N_TXT, IMG_BLK, embed_width).astype(jnp.bfloat16)
        image_delta = jnp.einsum('bie,ef->if', image_parts.astype(jnp.float32), image_out)
        new_top = jnp.maximum(col_top, lax.optimization_barrier(jnp.max(scores, axis=1)))
        new_sum = col_sum * jnp.exp(col_top - new_top) + lax.optimization_barrier(jnp.sum(jnp.exp(scores - new_top[:, None, :]), axis=1))
        return ((new_top, new_sum), image_delta)
    start_carry = (jnp.full((head_count, NT), MASKED, dtype=jnp.float32), jnp.zeros((head_count, NT), dtype=jnp.float32))
    scanned = lax.scan(first_pass, start_carry, query_blocks)
    col_top, col_sum = scanned[0]
    image_delta = scanned[1].reshape(NI, D)
    joined_image = (image_tokens.astype(jnp.float32) + image_layer_scale * image_delta).astype(jnp.bfloat16)

    def second_pass(prompt_delta, blocks):
        query_block, value_block = blocks
        scores = block_scores(query_block)
        col_exp = jnp.exp(scores - col_top[:, None, :])
        rounded = lax.optimization_barrier(col_exp.astype(jnp.bfloat16)).astype(jnp.float32)
        prompt_part = jnp.einsum('hit,ihd->thd', rounded, value_block.astype(jnp.float32)) / col_sum.T[:, :, None]
        prompt_part = prompt_part.reshape(NT, embed_width).astype(jnp.bfloat16)
        return (prompt_delta + jnp.dot(prompt_part.astype(jnp.float32), prompt_out_weight.astype(jnp.float32), preferred_element_type=jnp.float32), None)
    prompt_delta = lax.scan(second_pass, jnp.zeros((NT, D), dtype=jnp.float32), (query_blocks, image_value_blocks))[0]
    prompt_joined = prompt_tokens.astype(jnp.float32) + prompt_layer_scale * prompt_delta
    joined_prompt = prompt_joined.astype(jnp.bfloat16)
    members = jnp.logical_and(category_ids[None, :] == jnp.arange(CATS, dtype=jnp.int32)[:, None], prompt_valid[None, :] > 0).astype(jnp.float32)
    category_sum = jnp.dot(members, prompt_joined, precision=lax.Precision.HIGHEST)
    category_embed = category_sum / lax.optimization_barrier(jnp.sum(members, axis=1))[:, None]
    return (joined_image, joined_prompt, category_embed)
```

```python
import functools

import jax
import jax.numpy as jnp
from jax import lax
from jax.experimental import pallas as pl
from jax.experimental.pallas import tpu as pltpu
from jax.sharding import PartitionSpec as P

HD = 256
EPSILON = 1e-05
MASKED = -1e30
FLOOR = -1e29
WINDOW = 8
COUNT_BASE = 4096
MESH = pl.DeviceIdType.MESH
F32 = jnp.float32
BF16 = jnp.bfloat16


def normalize(tokens_in, gain_row):
    values = tokens_in.astype(F32)
    average = jnp.mean(values, axis=-1, keepdims=True)
    centered = values - average
    variance = jnp.mean(centered * centered, axis=-1, keepdims=True)
    return centered * lax.rsqrt(variance + EPSILON) * gain_row


def iota(shape, dim):
    return lax.broadcasted_iota(jnp.int32, shape, dim)


def mm(a, b):
    return jnp.dot(a, b, preferred_element_type=F32)


def mm_t(a, b):
    return lax.dot_general(a, b, (((1,), (1,)), ((), ())), preferred_element_type=F32)


def kernel(
    n_img, n_txt,
    img_ref, prompt_ref, ids_ref, valid_ref, igain_ref, pgain_ref,
    wq_hbm, wk_hbm, wvi_hbm, wvp_hbm, woi_hbm, wop_hbm, iscale_ref, pscale_ref,
    out_img, out_prompt, out_cat,
    wq, wk, wvi, wvp, woi, wop, xi, xp, meta, numer_i, numer_p, stat_r, stat_c,
    di_out, di_in, dp_out, dp_in, win,
    w_sem, xi_s, xi_r, xp_s, xp_r, meta_s, meta_r, sr_s, sr_r, sc_s, sc_r,
    di_s, di_r, dp_s, dp_r, win_s, win_r,
):
    n_dev = n_img * n_txt
    my_img, my_txt = lax.axis_index("img"), lax.axis_index("txt")
    me = my_img * n_txt + my_txt
    rows, width = img_ref.shape
    tokens = prompt_ref.shape[0]
    padded = xp.shape[1]
    embed = wq.shape[1]
    heads = embed // HD
    n_rows = n_txt * rows
    n_cols = n_img * padded

    weights = ((wk_hbm, wk), (wvp_hbm, wvp), (wq_hbm, wq), (wvi_hbm, wvi), (wop_hbm, wop), (woi_hbm, woi))
    loads = [pltpu.make_async_copy(src, dst, w_sem.at[n]) for n, (src, dst) in enumerate(weights)]
    for load in loads:
        load.start()

    barrier = pltpu.get_barrier_semaphore()

    def device(d):
        return {"img": d // n_txt, "txt": d % n_txt}

    @pl.loop(1, n_dev)
    def _(step):
        pl.semaphore_signal(barrier, inc=1, device_id=device(lax.rem(me + step, n_dev)), device_id_type=MESH)

    normed = normalize(prompt_ref[...], pgain_ref[...].reshape(1, width))
    valid_row = valid_ref[...].reshape(1, tokens)
    ids_row = ids_ref[...].reshape(1, tokens)
    diagonal = iota((tokens, tokens), 0) == iota((tokens, tokens), 1)
    valid_col = jnp.sum(jnp.where(diagonal, jnp.broadcast_to(valid_row, (tokens, tokens)).astype(F32), 0.0), axis=1, keepdims=True)
    place = my_img * padded
    spot = place % width + iota((tokens, width), 0) == iota((tokens, width), 1)
    mark_row = jnp.sum(jnp.where(spot, valid_col, 0.0), axis=0, keepdims=True)
    spare = padded - tokens
    marks = jnp.where(iota((spare, width), 0) == place // width, mark_row, 0.0)
    xp[my_img] = jnp.concatenate([normed, marks], axis=0).astype(BF16)

    rel = ids_row - ids_row[:, 0:1]
    members = jnp.logical_and(rel == iota((WINDOW, tokens), 0), valid_row > 0).astype(F32)
    counts = jnp.sum(members, axis=1, keepdims=True).astype(jnp.int32)
    lane = iota((WINDOW, 128), 1) - (me % 8) * 16
    slot = iota((WINDOW, 128), 0)
    mine = jnp.logical_and(jnp.logical_and(lane >= 0, lane < 16), lane % WINDOW == slot)
    value = counts * COUNT_BASE + ids_row[:, 0:1] + slot
    meta[me] = jnp.sum(jnp.where(mine, value, 0), axis=0, keepdims=True)

    xi[my_txt] = normalize(img_ref[...], igain_ref[...].reshape(1, width)).astype(BF16)

    def over_img(src, dst, s, r, p, to=None):
        return pltpu.make_async_remote_copy(src, dst, s.at[p], r.at[my_img], device_id={"img": p, "txt": my_txt}, device_id_type=MESH)

    def over_txt(src, dst, s, r, p):
        return pltpu.make_async_remote_copy(src, dst, s.at[p], r.at[my_txt], device_id={"img": my_img, "txt": p}, device_id_type=MESH)

    def gather_copy(buf, s, r, axis, p):
        mine_ = my_img if axis == "img" else my_txt
        make = over_img if axis == "img" else over_txt
        return make(buf.at[mine_], buf.at[mine_], s, r, p)

    def scatter_copy(out, into, s, r, axis, p):
        mine_ = my_img if axis == "img" else my_txt
        make = over_img if axis == "img" else over_txt
        return make(out.at[p], into.at[mine_], s, r, p)

    def arrived(buf, s, r, p):
        pltpu.make_async_remote_copy(buf.at[p], buf.at[p], s.at[p], r.at[p], device_id={"img": my_img, "txt": my_txt}, device_id_type=MESH).wait_recv()

    def others(axis, body):
        count, mine_ = (n_img, my_img) if axis == "img" else (n_txt, my_txt)

        @pl.loop(1, count)
        def _(step):
            body(lax.rem(mine_ + step, count))

    def everyone(body):
        @pl.loop(1, n_dev)
        def _(step):
            body(lax.rem(me + step, n_dev))

    def wide(buf, s, r, p):
        return pltpu.make_async_remote_copy(buf.at[me], buf.at[me], s.at[p], r.at[me], device_id=device(p), device_id_type=MESH)

    pl.semaphore_wait(barrier, n_dev - 1)

    others("txt", lambda p: gather_copy(xi, xi_s, xi_r, "txt", p).start())
    others("img", lambda p: gather_copy(xp, xp_s, xp_r, "img", p).start())
    everyone(lambda p: wide(meta, meta_s, meta_r, p).start())

    for load in loads[:4]:
        load.wait()
    others("img", lambda p: arrived(xp, xp_s, xp_r, p))
    others("txt", lambda p: arrived(xi, xi_s, xi_r, p))

    x_prompt = xp[...].reshape(n_cols, width)
    x_image = xi[...].reshape(n_rows, width)
    mark_rows = jnp.sum(xp[:, tokens:, :].astype(F32), axis=0)
    mask = jnp.concatenate([mark_rows[n : n + 1] for n in range(max(1, n_cols // width))], axis=1)[:, :n_cols] > 0.0

    def one_head(h, carry):
        row_stats, col_stats = carry
        part = pl.ds(pl.multiple_of(h * HD, HD), HD)
        k = mm(x_prompt, wk[:, part]).astype(BF16)
        q = (mm(x_image, wq[:, part]) * (HD ** -0.5)).astype(BF16)
        v_p = mm(x_prompt, wvp[:, part]).astype(BF16)
        v_i = mm(x_image, wvi[:, part]).astype(BF16)
        turned = mm_t(k, q)
        c_top = jnp.max(turned, axis=1, keepdims=True)
        c_exp = jnp.exp(turned - c_top)
        c_sum = jnp.sum(c_exp, axis=1, keepdims=True)
        numer_p[h] = mm(c_exp.astype(BF16), v_i)
        scores = jnp.where(mask, mm_t(q, k), MASKED)
        r_top = jnp.maximum(jnp.max(scores, axis=1, keepdims=True), FLOOR)
        r_exp = jnp.exp(scores - r_top)
        r_sum = jnp.sum(r_exp, axis=1, keepdims=True)
        numer_i[h] = mm(r_exp.astype(BF16), v_p)

        def put(stats, top, total):
            at = iota(stats.shape, 1)
            return jnp.where(at == h, top, jnp.where(at == heads + h, total, stats))

        return put(row_stats, r_top, r_sum), put(col_stats, c_top, c_sum)

    carry = (jnp.zeros((n_rows, 128), F32), jnp.zeros((n_cols, 128), F32))
    if n_cols <= 512:
        for h in range(heads):
            carry = one_head(h, carry)
    else:
        carry = lax.fori_loop(0, heads, one_head, carry)
    row_stats, col_stats = carry
    stat_c[my_img] = col_stats.T[: 2 * heads]
    others("img", lambda p: gather_copy(stat_c, sc_s, sc_r, "img", p).start())
    stat_r[my_txt] = row_stats.T[: 2 * heads]
    others("txt", lambda p: gather_copy(stat_r, sr_s, sr_r, "txt", p).start())

    def factor(buf, mine_):
        tops, sums = buf[:, :heads, :], buf[:, heads:, :]
        top = jnp.max(tops, axis=0)
        total = jnp.sum(sums * jnp.exp(tops - top[None]), axis=0)
        own = jnp.exp(buf[mine_][:heads] - top) / total
        return jnp.concatenate([own, jnp.zeros((128 - heads, own.shape[1]), F32)], axis=0).T

    for load in loads[4:]:
        load.wait()
    others("img", lambda p: arrived(stat_c, sc_s, sc_r, p))
    scale = factor(stat_c, my_img)
    delta = mm((numer_p[0] * scale[:, 0:1]).astype(BF16), wop[0:HD, :])
    for h in range(1, heads):
        delta += mm((numer_p[h] * scale[:, h : h + 1]).astype(BF16), wop[h * HD : (h + 1) * HD, :])
    dp_out[...] = delta.astype(BF16).reshape(dp_out.shape)
    dp_in[my_img] = dp_out[my_img]
    others("img", lambda p: scatter_copy(dp_out, dp_in, dp_s, dp_r, "img", p).start())

    others("txt", lambda p: arrived(stat_r, sr_s, sr_r, p))
    scale = factor(stat_r, my_txt)
    delta = mm((numer_i[0] * scale[:, 0:1]).astype(BF16), woi[0:HD, :])
    for h in range(1, heads):
        delta += mm((numer_i[h] * scale[:, h : h + 1]).astype(BF16), woi[h * HD : (h + 1) * HD, :])
    di_out[...] = delta.astype(BF16).reshape(di_out.shape)
    di_in[my_txt] = di_out[my_txt]
    others("txt", lambda p: scatter_copy(di_out, di_in, di_s, di_r, "txt", p).start())

    others("img", lambda p: arrived(dp_in, dp_s, dp_r, p))
    prompt_delta = jnp.sum(dp_in[...].astype(F32), axis=0)[:tokens]
    joined = prompt_ref[...].astype(F32) + pscale_ref[...].reshape(1, width) * prompt_delta
    out_prompt[...] = joined.astype(BF16)
    sums = jnp.dot(members, joined, precision=lax.Precision.HIGHEST, preferred_element_type=F32)
    win[me] = jnp.concatenate([sums[:, :128], sums[:, 128:]], axis=0).astype(BF16)
    everyone(lambda p: wide(win, win_s, win_r, p).start())

    others("txt", lambda p: arrived(di_in, di_s, di_r, p))
    image_delta = jnp.sum(di_in[...].astype(F32), axis=0)
    out_img[...] = (img_ref[...].astype(F32) + iscale_ref[...].reshape(1, width) * image_delta).astype(BF16)

    everyone(lambda p: arrived(meta, meta_s, meta_r, p))
    cats = out_cat.shape[0]
    groups = [jnp.sum(meta[g * 8 : g * 8 + 8], axis=0) for g in range(n_dev // 8)]
    packed = jnp.concatenate(groups, axis=1)
    key = jnp.broadcast_to(packed % COUNT_BASE, (cats, n_dev * 16)) == iota((cats, n_dev * 16), 0)
    first = iota((cats, n_dev * 16), 1) % 16 < WINDOW
    pick_lo = jnp.logical_and(key, first)
    pick_hi = jnp.logical_and(key, jnp.logical_not(first))
    tally = jnp.sum(jnp.where(pick_lo, (packed // COUNT_BASE).astype(F32), 0.0), axis=1, keepdims=True)
    pick_lo = jnp.where(pick_lo, 1.0, 0.0).astype(BF16)
    pick_hi = jnp.where(pick_hi, 1.0, 0.0).astype(BF16)

    everyone(lambda p: arrived(win, win_s, win_r, p))
    windows = win[...].reshape(n_dev * 16, 128)
    out_cat[:, :128] = mm(pick_lo, windows) / tally
    out_cat[:, 128:] = mm(pick_hi, windows) / tally

    others("txt", lambda p: gather_copy(xi, xi_s, xi_r, "txt", p).wait_send())
    others("img", lambda p: gather_copy(xp, xp_s, xp_r, "img", p).wait_send())
    everyone(lambda p: wide(meta, meta_s, meta_r, p).wait_send())
    others("img", lambda p: gather_copy(stat_c, sc_s, sc_r, "img", p).wait_send())
    others("txt", lambda p: gather_copy(stat_r, sr_s, sr_r, "txt", p).wait_send())
    others("img", lambda p: scatter_copy(dp_out, dp_in, dp_s, dp_r, "img", p).wait_send())
    others("txt", lambda p: scatter_copy(di_out, di_in, di_s, di_r, "txt", p).wait_send())
    everyone(lambda p: wide(win, win_s, win_r, p).wait_send())


def on_device(n_img, n_txt, image_tokens, prompt_tokens, *rest):
    n_dev = n_img * n_txt
    rows, width = image_tokens.shape
    tokens = prompt_tokens.shape[0]
    embed = rest[4].shape[1]
    heads = embed // HD
    padded = (tokens + 15) // 16 * 16
    n_rows, n_cols = n_txt * rows, n_img * padded
    cats = n_dev * tokens // 16
    vmem, hbm = pl.BlockSpec(memory_space=pltpu.VMEM), pl.BlockSpec(memory_space=pl.ANY)
    dma = pltpu.SemaphoreType.DMA
    return pl.pallas_call(
        functools.partial(kernel, n_img, n_txt),
        out_shape=(
            jax.ShapeDtypeStruct((rows, width), BF16),
            jax.ShapeDtypeStruct((tokens, width), BF16),
            jax.ShapeDtypeStruct((cats, width), F32),
        ),
        in_specs=[vmem] * 6 + [hbm] * 6 + [vmem] * 2,
        out_specs=(vmem, vmem, vmem),
        scratch_shapes=[
            pltpu.VMEM((width, embed), BF16),
            pltpu.VMEM((width, embed), BF16),
            pltpu.VMEM((width, embed), BF16),
            pltpu.VMEM((width, embed), BF16),
            pltpu.VMEM((embed, width), BF16),
            pltpu.VMEM((embed, width), BF16),
            pltpu.VMEM((n_txt, rows, width), BF16),
            pltpu.VMEM((n_img, padded, width), BF16),
            pltpu.VMEM((n_dev, 1, 128), jnp.int32),
            pltpu.VMEM((heads, n_rows, HD), F32),
            pltpu.VMEM((heads, n_cols, HD), F32),
            pltpu.VMEM((n_txt, 2 * heads, n_rows), F32),
            pltpu.VMEM((n_img, 2 * heads, n_cols), F32),
            pltpu.VMEM((n_txt, rows, width), BF16),
            pltpu.VMEM((n_txt, rows, width), BF16),
            pltpu.VMEM((n_img, padded, width), BF16),
            pltpu.VMEM((n_img, padded, width), BF16),
            pltpu.VMEM((n_dev, 16, 128), BF16),
            dma((6,)),
            dma((n_txt,)), dma((n_txt,)),
            dma((n_img,)), dma((n_img,)),
            dma((n_dev,)), dma((n_dev,)),
            dma((n_txt,)), dma((n_txt,)),
            dma((n_img,)), dma((n_img,)),
            dma((n_txt,)), dma((n_txt,)),
            dma((n_img,)), dma((n_img,)),
            dma((n_dev,)), dma((n_dev,)),
        ],
        compiler_params=pltpu.CompilerParams(
            collective_id=0, has_side_effects=True, vmem_limit_bytes=56 * 2**20
        ),
        name="joining_layer",
    )(image_tokens, prompt_tokens, *rest)


def solution(mesh):
    return jax.shard_map(
        functools.partial(on_device, mesh.shape["img"], mesh.shape["txt"]),
        mesh=mesh,
        in_specs=(
            P(("img", "txt"), None),
            P(("txt", "img"), None),
            P(("txt", "img")),
            P(("txt", "img")),
        )
        + (P(),) * 10,
        out_specs=(P(("img", "txt"), None), P(("txt", "img"), None), P()),
        check_vma=False,
    )
```

```python
import functools

import jax
import jax.numpy as jnp
from jax import lax
from jax.experimental import pallas as pl
from jax.experimental.pallas import tpu as pltpu
from jax.sharding import PartitionSpec as P

HD = 256
EPSILON = 1e-05
MASKED = -1e30
FLOOR = -1e29
WINDOW = 8
COUNT_BASE = 4096
MESH = pl.DeviceIdType.MESH
F32 = jnp.float32
BF16 = jnp.bfloat16


def normalize(tokens_in, gain_row):
    values = tokens_in.astype(F32)
    average = jnp.mean(values, axis=-1, keepdims=True)
    centered = values - average
    variance = jnp.mean(centered * centered, axis=-1, keepdims=True)
    return centered * lax.rsqrt(variance + EPSILON) * gain_row


def iota(shape, dim):
    return lax.broadcasted_iota(jnp.int32, shape, dim)


def mm(a, b):
    return jnp.dot(a, b, preferred_element_type=F32)


def mm_t(a, b):
    return lax.dot_general(a, b, (((1,), (1,)), ((), ())), preferred_element_type=F32)


def kernel(
    n_img, n_txt,
    img_ref, prompt_ref, ids_ref, valid_ref, igain_ref, pgain_ref,
    wq_hbm, wk_hbm, wvi_hbm, wvp_hbm, woi_hbm, wop_hbm, iscale_ref, pscale_ref,
    out_img, out_prompt, out_cat,
    wq, wk, wvi, wvp, woi, wop, xi, xp, meta, queries, keys, values_i, values_p, exp_c, exp_r,
    stat_r, stat_c, di_out, di_in, dp_out, dp_in, win, tally, cat,
    w_sem, xi_s, xi_r, xp_s, xp_r, meta_s, meta_r, sr_s, sr_r, sc_s, sc_r,
    di_s, di_r, dp_s, dp_r, win_s, win_r, tally_s, tally_r, cat_s, cat_r,
):
    my_img, my_txt = lax.axis_index("img"), lax.axis_index("txt")
    rows, width = img_ref.shape
    half = width // 2
    tokens = prompt_ref.shape[0]
    padded = xp.shape[1]
    embed = wq.shape[1]
    heads = embed // HD
    n_rows = n_txt * rows
    n_cols = n_img * padded
    cats = out_cat.shape[0]
    cat_lanes = tally.shape[2]

    weights = ((wq_hbm, wq), (wvi_hbm, wvi), (wk_hbm, wk), (wvp_hbm, wvp), (wop_hbm, wop), (woi_hbm, woi))
    loads = [pltpu.make_async_copy(src, dst, w_sem.at[n]) for n, (src, dst) in enumerate(weights)]
    for load in loads:
        load.start()

    def others(axis, body):
        count, mine = (n_img, my_img) if axis == "img" else (n_txt, my_txt)
        if count <= 8:
            for step in range(1, count):
                body(lax.rem(mine + step, count))
        else:

            @pl.loop(1, count)
            def _(step):
                body(lax.rem(mine + step, count))

    def place(axis, p):
        return {"img": p, "txt": my_txt} if axis == "img" else {"img": my_img, "txt": p}

    barrier = pltpu.get_barrier_semaphore()
    for axis in ("img", "txt"):
        others(axis, lambda p: pl.semaphore_signal(barrier, inc=1, device_id=place(axis, p), device_id_type=MESH))

    def send(axis, src, dst, s, r):
        mine = my_img if axis == "img" else my_txt
        others(
            axis,
            lambda p: pltpu.make_async_remote_copy(
                src(p), dst.at[mine], s.at[0], r.at[0], device_id=place(axis, p), device_id_type=MESH
            ).start(),
        )

    def whole(buf, s, r):
        part = buf.at[pl.ds(0, buf.shape[0] - 1)]
        return pltpu.make_async_remote_copy(
            part, part, s.at[0], r.at[0], device_id={"img": my_img, "txt": my_txt}, device_id_type=MESH
        )

    normed = normalize(prompt_ref[...], pgain_ref[...].reshape(1, width))
    valid_row = valid_ref[...].reshape(1, tokens)
    ids_row = ids_ref[...].reshape(1, tokens)
    diagonal = iota((tokens, tokens), 0) == iota((tokens, tokens), 1)
    valid_col = jnp.sum(jnp.where(diagonal, jnp.broadcast_to(valid_row, (tokens, tokens)).astype(F32), 0.0), axis=1, keepdims=True)
    spot_start = my_img * padded
    spot = spot_start % width + iota((tokens, width), 0) == iota((tokens, width), 1)
    mark_row = jnp.sum(jnp.where(spot, valid_col, 0.0), axis=0, keepdims=True)
    spare = padded - tokens
    marks = jnp.where(iota((spare, width), 0) == spot_start // width, mark_row, 0.0)
    xp[my_img] = jnp.concatenate([normed, marks], axis=0).astype(BF16)

    first_id = ids_row[:, 0:1]
    members = jnp.logical_and(ids_row - first_id == iota((WINDOW, tokens), 0), valid_row > 0).astype(F32)
    counts = jnp.sum(members, axis=1, keepdims=True).astype(jnp.int32)
    lane = iota((WINDOW, 128), 1) - (my_img % 8) * 16
    slot = iota((WINDOW, 128), 0)
    own_lane = jnp.logical_and(jnp.logical_and(lane >= 0, lane < 16), lane % WINDOW == slot)
    meta[my_img] = jnp.sum(jnp.where(own_lane, counts * COUNT_BASE + first_id + slot, 0), axis=0, keepdims=True)

    xi[my_txt] = normalize(img_ref[...], igain_ref[...].reshape(1, width)).astype(BF16)

    pl.semaphore_wait(barrier, n_img - 1 + n_txt - 1)

    def image_copy(p, at):
        return pltpu.make_async_remote_copy(
            xi.at[at], xi.at[at], xi_s.at[p], xi_r.at[at], device_id=place("txt", p), device_id_type=MESH
        )

    others("txt", lambda p: image_copy(p, my_txt).start())
    send("img", lambda p: xp.at[my_img], xp, xp_s, xp_r)
    send("img", lambda p: meta.at[my_img], meta, meta_s, meta_r)

    def project_image(p):
        at = pl.ds(pl.multiple_of(p * rows, rows), rows)
        queries[at, :] = (mm(xi[p], wq[...]) * (HD ** -0.5)).astype(BF16)
        values_i[at, :] = mm(xi[p], wvi[...]).astype(BF16)

    loads[0].wait()
    loads[1].wait()
    project_image(my_txt)
    loads[2].wait()
    loads[3].wait()
    whole(xp, xp_s, xp_r).wait_recv()
    x_prompt = xp[...].reshape(n_cols, width)
    keys[...] = mm(x_prompt, wk[...]).astype(BF16)
    values_p[...] = mm(x_prompt, wvp[...]).astype(BF16)
    mark_rows = jnp.sum(xp[:, tokens:, :].astype(F32), axis=0)
    mask = jnp.concatenate([mark_rows[n : n + 1] for n in range(max(1, n_cols // width))], axis=1)[:, :n_cols] > 0.0

    def take_image(p):
        image_copy(p, p).wait_recv()
        project_image(p)

    others("txt", take_image)

    def over_heads(body, stats):
        if n_cols <= 512:
            for h in range(heads):
                stats = body(h, stats)
            return stats
        return lax.fori_loop(0, heads, body, stats)

    def head(h):
        return pl.ds(h * HD, HD) if isinstance(h, int) else pl.ds(pl.multiple_of(h * HD, HD), HD)

    def put(h, stats, top, total):
        at = iota(stats.shape, 1)
        return jnp.where(at == h, top, jnp.where(at == heads + h, total, stats))

    def column_head(h, stats):
        scores = mm_t(keys[:, head(h)], queries[:, head(h)])
        top = jnp.max(scores, axis=1, keepdims=True)
        exps = jnp.exp(scores - top)
        exp_c[h] = exps.astype(BF16)
        return put(h, stats, top, jnp.sum(exps, axis=1, keepdims=True))

    def row_head(h, stats):
        scores = jnp.where(mask, mm_t(queries[:, head(h)], keys[:, head(h)]), MASKED)
        top = jnp.maximum(jnp.max(scores, axis=1, keepdims=True), FLOOR)
        exps = jnp.exp(scores - top)
        exp_r[h] = exps.astype(BF16)
        return put(h, stats, top, jnp.sum(exps, axis=1, keepdims=True))

    stats = over_heads(column_head, jnp.zeros((n_cols, 128), F32))
    stat_c[my_img] = stats.T[: 2 * heads]
    send("img", lambda p: stat_c.at[my_img], stat_c, sc_s, sc_r)
    stats = over_heads(row_head, jnp.zeros((n_rows, 128), F32))
    stat_r[my_txt] = stats.T[: 2 * heads]
    send("txt", lambda p: stat_r.at[my_txt], stat_r, sr_s, sr_r)

    def factor(buf, mine):
        tops, sums = buf[:, :heads, :], buf[:, heads:, :]
        top = jnp.max(tops, axis=0)
        total = jnp.sum(sums * jnp.exp(tops - top[None]), axis=0)
        own = jnp.exp(buf[mine][:heads] - top) / total
        return jnp.concatenate([own, jnp.zeros((128 - heads, own.shape[1]), F32)], axis=0).T

    def update(exps, values, scale_of, out_weight):
        numers = [mm(exps[h], values[:, head(h)]) for h in range(heads)]
        scale = scale_of()
        delta = 0.0
        for h in range(heads):
            delta += mm((numers[h] * scale[:, h : h + 1]).astype(BF16), out_weight[head(h), :])
        return delta.astype(BF16)

    def prompt_scale():
        loads[4].wait()
        whole(stat_c, sc_s, sc_r).wait_recv()
        return factor(stat_c, my_img)

    dp_out[...] = update(exp_c, values_i, prompt_scale, wop).reshape(dp_out.shape)
    dp_in[my_img] = dp_out[my_img]
    send("img", lambda p: dp_out.at[p], dp_in, dp_s, dp_r)

    whole(meta, meta_s, meta_r).wait_recv()
    packed = jnp.concatenate([jnp.sum(meta[g * 8 : g * 8 + 8], axis=0) for g in range(n_img // 8)], axis=1)
    key = jnp.broadcast_to(packed % COUNT_BASE, (cat_lanes, n_img * 16)) == iota((cat_lanes, n_img * 16), 0)
    low = iota((cat_lanes, n_img * 16), 1) % 16 < WINDOW
    pick_lo = jnp.where(jnp.logical_and(key, low), 1.0, 0.0).astype(BF16)
    pick_hi = jnp.where(jnp.logical_and(key, jnp.logical_not(low)), 1.0, 0.0).astype(BF16)
    numbers = jnp.broadcast_to((packed // COUNT_BASE).astype(F32), (8, n_img * 16)).astype(BF16)
    tally[my_txt] = mm_t(numbers, pick_lo)
    send("txt", lambda p: tally.at[my_txt], tally, tally_s, tally_r)

    def image_scale():
        loads[5].wait()
        whole(stat_r, sr_s, sr_r).wait_recv()
        return factor(stat_r, my_txt)

    di_out[...] = update(exp_r, values_p, image_scale, woi).reshape(di_out.shape)
    di_in[my_txt] = di_out[my_txt]
    send("txt", lambda p: di_out.at[p], di_in, di_s, di_r)

    whole(dp_in, dp_s, dp_r).wait_recv()
    prompt_delta = jnp.sum(dp_in[...].astype(F32), axis=0)[:tokens]
    joined = prompt_ref[...].astype(F32) + pscale_ref[...].reshape(1, width) * prompt_delta
    sums = jnp.dot(members, joined, precision=lax.Precision.HIGHEST, preferred_element_type=F32)
    win[my_img] = jnp.concatenate([sums[:, :half], sums[:, half:]], axis=0).astype(BF16)
    send("img", lambda p: win.at[my_img], win, win_s, win_r)
    out_prompt[...] = joined.astype(BF16)

    whole(di_in, di_s, di_r).wait_recv()
    image_delta = jnp.sum(di_in[...].astype(F32), axis=0)
    out_img[...] = (img_ref[...].astype(F32) + iscale_ref[...].reshape(1, width) * image_delta).astype(BF16)

    whole(win, win_s, win_r).wait_recv()
    windows = win[...].reshape(n_img * 16, half)
    block = jnp.concatenate([mm(pick_lo[:cats], windows), mm(pick_hi[:cats], windows)], axis=1)
    cat[my_txt] = block.astype(BF16)
    send("txt", lambda p: cat.at[my_txt], cat, cat_s, cat_r)

    whole(tally, tally_s, tally_r).wait_recv()
    tally_row = jnp.sum(tally[...], axis=0)[0:1]
    on_diagonal = iota((cats, cat_lanes), 0) == iota((cats, cat_lanes), 1)
    tally_col = jnp.sum(jnp.where(on_diagonal, tally_row, 0.0), axis=1, keepdims=True)
    whole(cat, cat_s, cat_r).wait_recv()
    out_cat[...] = jnp.sum(cat[...].astype(F32), axis=0) / tally_col

    others("txt", lambda p: image_copy(p, my_txt).wait_send())
    for buf, s, r in (
        (xp, xp_s, xp_r), (meta, meta_s, meta_r), (stat_c, sc_s, sc_r), (stat_r, sr_s, sr_r), (dp_in, dp_s, dp_r),
        (tally, tally_s, tally_r), (di_in, di_s, di_r), (win, win_s, win_r), (cat, cat_s, cat_r),
    ):
        whole(buf, s, r).wait_send()


def keep(*refs):
    count = len(refs) // 2
    sems = refs[-1]
    copies = [pltpu.make_async_copy(refs[n], refs[count + n], sems.at[n]) for n in range(count)]
    for copy in copies:
        copy.start()
    for copy in copies:
        copy.wait()


def on_device(n_img, n_txt, image_tokens, prompt_tokens, *rest):
    rows, width = image_tokens.shape
    tokens = prompt_tokens.shape[0]
    embed = rest[4].shape[1]
    heads = embed // HD
    padded = (tokens + 15) // 16 * 16
    n_rows, n_cols = n_txt * rows, n_img * padded
    cats = n_img * n_txt * tokens // 16
    cat_lanes = (cats + 127) // 128 * 128
    vmem, hbm = pl.BlockSpec(memory_space=pltpu.VMEM), pl.BlockSpec(memory_space=pl.ANY)
    dma = pltpu.SemaphoreType.DMA
    one = (dma((1,)), dma((1,)))
    outs = (
        jax.ShapeDtypeStruct((rows, width), BF16),
        jax.ShapeDtypeStruct((tokens, width), BF16),
        jax.ShapeDtypeStruct((cats, width), F32),
    )
    results = pl.pallas_call(
        functools.partial(kernel, n_img, n_txt),
        out_shape=outs,
        in_specs=[vmem] * 6 + [hbm] * 6 + [vmem] * 2,
        out_specs=(vmem, vmem, vmem),
        scratch_shapes=[pltpu.VMEM((width, embed), BF16)] * 4
        + [pltpu.VMEM((embed, width), BF16)] * 2
        + [
            pltpu.VMEM((n_txt, rows, width), BF16),
            pltpu.VMEM((n_img, padded, width), BF16),
            pltpu.VMEM((n_img, 1, 128), jnp.int32),
            pltpu.VMEM((n_rows, embed), BF16),
            pltpu.VMEM((n_cols, embed), BF16),
            pltpu.VMEM((n_rows, embed), BF16),
            pltpu.VMEM((n_cols, embed), BF16),
            pltpu.VMEM((heads, n_cols, n_rows), BF16),
            pltpu.VMEM((heads, n_rows, n_cols), BF16),
            pltpu.VMEM((n_txt, 2 * heads, n_rows), F32),
            pltpu.VMEM((n_img, 2 * heads, n_cols), F32),
            pltpu.VMEM((n_txt, rows, width), BF16),
            pltpu.VMEM((n_txt, rows, width), BF16),
            pltpu.VMEM((n_img, padded, width), BF16),
            pltpu.VMEM((n_img, padded, width), BF16),
            pltpu.VMEM((n_img, 16, width // 2), BF16),
            pltpu.VMEM((n_txt, 8, cat_lanes), F32),
            pltpu.VMEM((n_txt, cats, width), BF16),
            dma((6,)),
            dma((n_txt,)),
            dma((n_txt,)),
            *one, *one, *one, *one, *one, *one, *one, *one, *one,
        ],
        compiler_params=pltpu.CompilerParams(
            collective_id=0, has_side_effects=True, vmem_limit_bytes=56 * 2**20
        ),
        name="joining_layer",
    )(image_tokens, prompt_tokens, *rest)
    return pl.pallas_call(
        keep,
        out_shape=outs,
        in_specs=[hbm] * len(outs),
        out_specs=(hbm,) * len(outs),
        scratch_shapes=[dma((len(outs),))],
        name="keep",
    )(*results)


def solution(mesh):
    return jax.shard_map(
        functools.partial(on_device, mesh.shape["img"], mesh.shape["txt"]),
        mesh=mesh,
        in_specs=(
            P(("img", "txt"), None),
            P(("txt", "img"), None),
            P(("txt", "img")),
            P(("txt", "img")),
        )
        + (P(),) * 10,
        out_specs=(P(("img", "txt"), None), P(("txt", "img"), None), P()),
        check_vma=False,
    )
```

```python
import functools

import jax
import jax.numpy as jnp
from jax import lax
from jax.experimental import pallas as pl
from jax.experimental.pallas import tpu as pltpu
from jax.sharding import PartitionSpec as P

HD = 256
EPSILON = 1e-05
MASKED = -1e30
FLOOR = -1e29
WINDOW = 8
COUNT_BASE = 4096
TILE = 16
MESH = pl.DeviceIdType.MESH
F32 = jnp.float32
BF16 = jnp.bfloat16


def normalize(tokens_in, gain_row):
    values = tokens_in.astype(F32)
    average = jnp.mean(values, axis=-1, keepdims=True)
    centered = values - average
    variance = jnp.mean(centered * centered, axis=-1, keepdims=True)
    return centered * lax.rsqrt(variance + EPSILON) * gain_row


def iota(shape, dim):
    return lax.broadcasted_iota(jnp.int32, shape, dim)


def fold(block):
    extra = block[TILE:]
    half = block.shape[1] // 2
    return jnp.concatenate([block[:TILE], jnp.concatenate([extra[:, :half], extra[:, half:]], axis=0)], axis=1)


def mm(a, b):
    return jnp.dot(a, b, preferred_element_type=F32)


def mm_t(a, b):
    return lax.dot_general(a, b, (((1,), (1,)), ((), ())), preferred_element_type=F32)


def kernel(
    n_img, n_txt,
    img_hbm, prompt_hbm, ids_hbm, valid_hbm, igain_hbm, pgain_hbm,
    wq_hbm, wk_hbm, wvi_hbm, wvp_hbm, woi_hbm, wop_hbm, iscale_hbm, pscale_hbm,
    out_img, out_prompt, out_cat,
    img_ref, prompt_ref, ids_ref, valid_ref, igain_ref, pgain_ref, iscale_ref, pscale_ref,
    wq, wk, wvi, wvp, woi, wop, xi, xp, meta, queries, keys, values_i, values_p, exp_c, exp_r,
    stat_r, stat_c, di_out, di_in, dp_out, dp_in, win, tally, cat,
    in_sem, w_sem, xi_s, xi_r, relay_s, xp_s, xp_r, meta_s, meta_r, sr_s, sr_r, sc_s, sc_r,
    di_s, di_r, dp_s, dp_r, win_s, win_r, tally_s, tally_r, cat_s, cat_r,
):
    my_img, my_txt = lax.axis_index("img"), lax.axis_index("txt")
    rows, width = img_ref.shape
    half = width // 2
    tokens = prompt_ref.shape[0]
    spare = tokens - TILE
    embed = wq.shape[1]
    heads = embed // HD
    n_rows = n_txt * rows
    n_cols = n_img * tokens
    cats = out_cat.shape[0]
    cat_lanes = tally.shape[2]

    inputs = (
        (prompt_hbm, prompt_ref), (pgain_hbm, pgain_ref), (valid_hbm, valid_ref), (ids_hbm, ids_ref),
        (img_hbm, img_ref), (igain_hbm, igain_ref), (iscale_hbm, iscale_ref), (pscale_hbm, pscale_ref),
    )
    fetches = [pltpu.make_async_copy(src, dst, in_sem.at[n]) for n, (src, dst) in enumerate(inputs)]
    weights = ((wq_hbm, wq), (wvi_hbm, wvi), (wk_hbm, wk), (wvp_hbm, wvp), (wop_hbm, wop), (woi_hbm, woi))
    loads = [pltpu.make_async_copy(src, dst, w_sem.at[n]) for n, (src, dst) in enumerate(weights)]
    for fetch in fetches:
        fetch.start()

    def others(axis, body):
        count, mine = (n_img, my_img) if axis == "img" else (n_txt, my_txt)
        if count <= 8:
            for step in range(1, count):
                body(lax.rem(mine + step, count))
        else:

            @pl.loop(1, count)
            def _(step):
                body(lax.rem(mine + step, count))

    def place(axis, p):
        return {"img": p, "txt": my_txt} if axis == "img" else {"img": my_img, "txt": p}

    barrier = pltpu.get_barrier_semaphore()
    for axis in ("img", "txt"):
        others(axis, lambda p: pl.semaphore_signal(barrier, inc=1, device_id=place(axis, p), device_id_type=MESH))
    for load in loads:
        load.start()

    def send(axis, src, dst, s, r):
        mine = my_img if axis == "img" else my_txt
        others(
            axis,
            lambda p: pltpu.make_async_remote_copy(
                src(p), dst.at[mine], s.at[0], r.at[0], device_id=place(axis, p), device_id_type=MESH
            ).start(),
        )

    def whole(buf, s, r):
        part = buf.at[pl.ds(0, buf.shape[0] - 1)]
        return pltpu.make_async_remote_copy(
            part, part, s.at[0], r.at[0], device_id={"img": my_img, "txt": my_txt}, device_id_type=MESH
        )

    for fetch in fetches[:4]:
        fetch.wait()
    xp[my_img] = fold(normalize(prompt_ref[...], pgain_ref[...].reshape(1, width))).astype(BF16)

    valid_row = valid_ref[...].reshape(1, tokens)
    ids_row = ids_ref[...].reshape(1, tokens)
    first_id = ids_row[:, 0:1]
    members = jnp.logical_and(ids_row - first_id == iota((WINDOW, tokens), 0), valid_row > 0).astype(F32)
    counts = jnp.sum(members, axis=1, keepdims=True).astype(jnp.int32)
    lane = iota((WINDOW, 128), 1) - (my_img % 8) * TILE
    slot = iota((WINDOW, 128), 0)
    own_lane = jnp.logical_and(jnp.logical_and(lane >= 0, lane < TILE), lane % WINDOW == slot)
    numbers = jnp.sum(jnp.where(own_lane, counts * COUNT_BASE + first_id + slot, 0), axis=0, keepdims=True)
    diagonal = iota((tokens, tokens), 0) == iota((tokens, tokens), 1)
    valid_col = jnp.sum(jnp.where(diagonal, jnp.broadcast_to(valid_row, (tokens, tokens)), 0), axis=1, keepdims=True)

    def marks(at, first, count):
        here = at + iota((count, 128), 0) == iota((count, 128), 1)
        return jnp.sum(jnp.where(here, valid_col[first : first + count], 0), axis=0, keepdims=True)

    meta[my_img] = jnp.concatenate(
        [numbers, marks((my_img % 8) * TILE, 0, TILE), marks((my_img % (128 // spare)) * spare, TILE, spare)], axis=1
    )

    fetches[4].wait()
    fetches[5].wait()
    xi[my_txt] = normalize(img_ref[...], igain_ref[...].reshape(1, width)).astype(BF16)

    pl.semaphore_wait(barrier, n_img - 1 + n_txt - 1)

    def image_copy(p, at):
        return pltpu.make_async_remote_copy(
            xi.at[at], xi.at[at], xi_s.at[p], xi_r.at[at], device_id=place("txt", p), device_id_type=MESH
        )

    mate = my_txt + 1 - 2 * (my_txt % 2)
    far = [lax.rem(my_txt + 2 * step, n_txt) for step in range(1, n_txt // 2)]
    send("img", lambda p: xp.at[my_img], xp, xp_s, xp_r)
    for p in far:
        image_copy(p, my_txt).start()
    image_copy(mate, my_txt).start()
    send("img", lambda p: meta.at[my_img], meta, meta_s, meta_r)

    def project_image(p):
        at = pl.ds(pl.multiple_of(p * rows, rows), rows)
        queries[at, :] = (mm(xi[p], wq[...]) * (HD ** -0.5)).astype(BF16)
        values_i[at, :] = mm(xi[p], wvi[...]).astype(BF16)

    loads[0].wait()
    loads[1].wait()
    project_image(my_txt)
    loads[2].wait()
    loads[3].wait()
    whole(xp, xp_s, xp_r).wait_recv()
    tall = xp[:, :, :width].reshape(n_img * TILE, width)
    short = xp[:, :, width:].astype(F32)
    short = jnp.concatenate([short[:, :spare], short[:, spare:]], axis=2).reshape(n_img * spare, width)
    x_prompt = jnp.concatenate([tall, short.astype(BF16)], axis=0)
    keys[...] = mm(x_prompt, wk[...]).astype(BF16)
    values_p[...] = mm(x_prompt, wvp[...]).astype(BF16)

    def relay(p):
        return pltpu.make_async_remote_copy(
            xi.at[p], xi.at[p], relay_s.at[p], xi_r.at[p], device_id=place("txt", mate), device_id_type=MESH
        )

    for p in far:
        image_copy(p, p).wait_recv()
        relay(p).start()
    image_copy(mate, mate).wait_recv()
    project_image(mate)
    for p in far:
        project_image(p)

    whole(meta, meta_s, meta_r).wait_recv()
    per = 128 // spare
    tall_marks = [jnp.sum(meta[g * 8 : g * 8 + 8, :, 128:256], axis=0) for g in range(n_img // 8)]
    short_marks = [jnp.sum(meta[g : min(g + per, n_img), :, 256:], axis=0) for g in range(0, n_img, per)]
    mask = jnp.concatenate(tall_marks + short_marks, axis=1)[:, :n_cols] > 0

    for p in far:
        there = p + 1 - 2 * (p % 2)
        image_copy(there, there).wait_recv()
        project_image(there)

    def over_heads(body, stats):
        if n_cols <= 512:
            for h in range(heads):
                stats = body(h, stats)
            return stats
        return lax.fori_loop(0, heads, body, stats)

    def head(h):
        return pl.ds(h * HD, HD) if isinstance(h, int) else pl.ds(pl.multiple_of(h * HD, HD), HD)

    def put(h, stats, top, total):
        at = iota(stats.shape, 1)
        return jnp.where(at == h, top, jnp.where(at == heads + h, total, stats))

    def column_head(h, stats):
        scores = mm_t(keys[:, head(h)], queries[:, head(h)])
        top = jnp.max(scores, axis=1, keepdims=True)
        exps = jnp.exp(scores - top)
        exp_c[h] = exps.astype(BF16)
        return put(h, stats, top, jnp.sum(exps, axis=1, keepdims=True))

    def row_head(h, stats):
        scores = jnp.where(mask, mm_t(queries[:, head(h)], keys[:, head(h)]), MASKED)
        top = jnp.maximum(jnp.max(scores, axis=1, keepdims=True), FLOOR)
        exps = jnp.exp(scores - top)
        exp_r[h] = exps.astype(BF16)
        return put(h, stats, top, jnp.sum(exps, axis=1, keepdims=True))

    stats = over_heads(column_head, jnp.zeros((n_cols, 128), F32))
    stat_c[my_img] = stats.T[: 2 * heads]
    send("img", lambda p: stat_c.at[my_img], stat_c, sc_s, sc_r)
    stats = over_heads(row_head, jnp.zeros((n_rows, 128), F32))
    stat_r[my_txt] = stats.T[: 2 * heads]
    send("txt", lambda p: stat_r.at[my_txt], stat_r, sr_s, sr_r)

    def factor(buf, mine):
        tops, sums = buf[:, :heads, :], buf[:, heads:, :]
        top = jnp.max(tops, axis=0)
        total = jnp.sum(sums * jnp.exp(tops - top[None]), axis=0)
        own = jnp.exp(buf[mine][:heads] - top) / total
        return jnp.concatenate([own, jnp.zeros((128 - heads, own.shape[1]), F32)], axis=0).T

    def update(exps, values, scale_of, out_weight):
        numers = [mm(exps[h], values[:, head(h)]) for h in range(heads)]
        scale = scale_of()
        delta = 0.0
        for h in range(heads):
            delta += mm((numers[h] * scale[:, h : h + 1]).astype(BF16), out_weight[head(h), :])
        return delta

    def prompt_scale():
        loads[4].wait()
        whole(stat_c, sc_s, sc_r).wait_recv()
        return factor(stat_c, my_img)

    delta = update(exp_c, values_i, prompt_scale, wop)
    tall = delta[: n_img * TILE].reshape(n_img, TILE, width)
    short = delta[n_img * TILE :].reshape(n_img, spare, width)
    short = jnp.concatenate([short[:, :, :half], short[:, :, half:]], axis=1)
    dp_out[...] = jnp.concatenate([tall, short], axis=2).astype(BF16)
    dp_in[my_img] = dp_out[my_img]
    send("img", lambda p: dp_out.at[p], dp_in, dp_s, dp_r)

    packed = jnp.concatenate([jnp.sum(meta[g * 8 : g * 8 + 8, :, :128], axis=0) for g in range(n_img // 8)], axis=1)
    key = jnp.broadcast_to(packed % COUNT_BASE, (cat_lanes, n_img * 16)) == iota((cat_lanes, n_img * 16), 0)
    low = iota((cat_lanes, n_img * 16), 1) % 16 < WINDOW
    pick_lo = jnp.where(jnp.logical_and(key, low), 1.0, 0.0).astype(BF16)
    pick_hi = jnp.where(jnp.logical_and(key, jnp.logical_not(low)), 1.0, 0.0).astype(BF16)
    numbers = jnp.broadcast_to((packed // COUNT_BASE).astype(F32), (8, n_img * 16)).astype(BF16)
    tally[my_txt] = mm_t(numbers, pick_lo)
    send("txt", lambda p: tally.at[my_txt], tally, tally_s, tally_r)

    def image_scale():
        loads[5].wait()
        whole(stat_r, sr_s, sr_r).wait_recv()
        return factor(stat_r, my_txt)

    di_out[...] = update(exp_r, values_p, image_scale, woi).astype(BF16).reshape(di_out.shape)
    di_in[my_txt] = di_out[my_txt]
    send("txt", lambda p: di_out.at[p], di_in, di_s, di_r)

    whole(dp_in, dp_s, dp_r).wait_recv()
    total = jnp.sum(dp_in[...].astype(F32), axis=0)
    short = jnp.concatenate([total[:spare, width:], total[spare:, width:]], axis=1)
    prompt_delta = jnp.concatenate([total[:, :width], short], axis=0)
    fetches[6].wait()
    fetches[7].wait()
    joined = prompt_ref[...].astype(F32) + pscale_ref[...].reshape(1, width) * prompt_delta
    sums = jnp.dot(members, joined, precision=lax.Precision.HIGHEST, preferred_element_type=F32)
    win[my_img] = jnp.concatenate([sums[:, :half], sums[:, half:]], axis=0).astype(BF16)
    send("img", lambda p: win.at[my_img], win, win_s, win_r)
    out_prompt[...] = joined.astype(BF16)

    whole(di_in, di_s, di_r).wait_recv()
    image_delta = jnp.sum(di_in[...].astype(F32), axis=0)
    out_img[...] = (img_ref[...].astype(F32) + iscale_ref[...].reshape(1, width) * image_delta).astype(BF16)

    whole(win, win_s, win_r).wait_recv()
    windows = win[...].reshape(n_img * 16, half)
    block = jnp.concatenate([mm(pick_lo[:cats], windows), mm(pick_hi[:cats], windows)], axis=1)
    cat[my_txt] = block.astype(BF16)
    send("txt", lambda p: cat.at[my_txt], cat, cat_s, cat_r)

    whole(tally, tally_s, tally_r).wait_recv()
    tally_row = jnp.sum(tally[...], axis=0)[0:1]
    on_diagonal = iota((cats, cat_lanes), 0) == iota((cats, cat_lanes), 1)
    tally_col = jnp.sum(jnp.where(on_diagonal, tally_row, 0.0), axis=1, keepdims=True)
    whole(cat, cat_s, cat_r).wait_recv()
    out_cat[...] = jnp.sum(cat[...].astype(F32), axis=0) / tally_col

    for p in far:
        image_copy(p, my_txt).wait_send()
        relay(p).wait_send()
    image_copy(mate, my_txt).wait_send()
    for buf, s, r in (
        (xp, xp_s, xp_r), (meta, meta_s, meta_r), (stat_c, sc_s, sc_r), (stat_r, sr_s, sr_r), (dp_in, dp_s, dp_r),
        (tally, tally_s, tally_r), (di_in, di_s, di_r), (win, win_s, win_r), (cat, cat_s, cat_r),
    ):
        whole(buf, s, r).wait_send()


def keep(*refs):
    count = len(refs) // 2
    for n in range(count):
        refs[count + n][...] = refs[n][...]


def on_device(n_img, n_txt, image_tokens, prompt_tokens, *rest):
    rows, width = image_tokens.shape
    tokens = prompt_tokens.shape[0]
    embed = rest[4].shape[1]
    heads = embed // HD
    n_rows, n_cols = n_txt * rows, n_img * tokens
    folded = width + width // 2
    cats = n_img * n_txt * tokens // 16
    cat_lanes = (cats + 127) // 128 * 128
    vmem, hbm = pl.BlockSpec(memory_space=pltpu.VMEM), pl.BlockSpec(memory_space=pl.ANY)
    dma = pltpu.SemaphoreType.DMA
    one = (dma((1,)), dma((1,)))
    outs = (
        jax.ShapeDtypeStruct((rows, width), BF16),
        jax.ShapeDtypeStruct((tokens, width), BF16),
        jax.ShapeDtypeStruct((cats, width), F32),
    )
    results = pl.pallas_call(
        functools.partial(kernel, n_img, n_txt),
        out_shape=tuple(pltpu.VMEM(out.shape, out.dtype) for out in outs),
        in_specs=[hbm] * 14,
        out_specs=(vmem, vmem, vmem),
        scratch_shapes=[pltpu.VMEM(x.shape, x.dtype) for x in (image_tokens, prompt_tokens, *rest[:4], *rest[10:])]
        + [pltpu.VMEM((width, embed), BF16)] * 4
        + [pltpu.VMEM((embed, width), BF16)] * 2
        + [
            pltpu.VMEM((n_txt, rows, width), BF16),
            pltpu.VMEM((n_img, TILE, folded), BF16),
            pltpu.VMEM((n_img, 1, 384), jnp.int32),
            pltpu.VMEM((n_rows, embed), BF16),
            pltpu.VMEM((n_cols, embed), BF16),
            pltpu.VMEM((n_rows, embed), BF16),
            pltpu.VMEM((n_cols, embed), BF16),
            pltpu.VMEM((heads, n_cols, n_rows), BF16),
            pltpu.VMEM((heads, n_rows, n_cols), BF16),
            pltpu.VMEM((n_txt, 2 * heads, n_rows), F32),
            pltpu.VMEM((n_img, 2 * heads, n_cols), F32),
            pltpu.VMEM((n_txt, rows, width), BF16),
            pltpu.VMEM((n_txt, rows, width), BF16),
            pltpu.VMEM((n_img, TILE, folded), BF16),
            pltpu.VMEM((n_img, TILE, folded), BF16),
            pltpu.VMEM((n_img, 16, width // 2), BF16),
            pltpu.VMEM((n_txt, 8, cat_lanes), F32),
            pltpu.VMEM((n_txt, cats, width), BF16),
            dma((8,)),
            dma((6,)),
            dma((n_txt,)),
            dma((n_txt,)),
            dma((n_txt,)),
            *one, *one, *one, *one, *one, *one, *one, *one, *one,
        ],
        compiler_params=pltpu.CompilerParams(
            collective_id=0, has_side_effects=True, vmem_limit_bytes=56 * 2**20
        ),
        name="joining_layer",
    )(image_tokens, prompt_tokens, *rest)
    return pl.pallas_call(
        keep,
        out_shape=outs,
        in_specs=[vmem] * len(outs),
        out_specs=(vmem,) * len(outs),
        compiler_params=pltpu.CompilerParams(vmem_limit_bytes=2**20),
        name="keep",
    )(*results)


def solution(mesh):
    return jax.shard_map(
        functools.partial(on_device, mesh.shape["img"], mesh.shape["txt"]),
        mesh=mesh,
        in_specs=(
            P(("img", "txt"), None),
            P(("txt", "img"), None),
            P(("txt", "img")),
            P(("txt", "img")),
        )
        + (P(),) * 10,
        out_specs=(P(("img", "txt"), None), P(("txt", "img"), None), P()),
        check_vma=False,
    )
```

```python
import functools

import jax
import jax.numpy as jnp
from jax import lax
from jax.experimental import pallas as pl
from jax.experimental.pallas import tpu as pltpu
from jax.sharding import PartitionSpec as P

HD = 256
EPSILON = 1e-05
MASKED = -1e30
FLOOR = -1e29
WINDOW = 8
COUNT_BASE = 4096
TILE = 16
MESH = pl.DeviceIdType.MESH
F32 = jnp.float32
BF16 = jnp.bfloat16


def normalize(tokens_in, gain_row):
    values = tokens_in.astype(F32)
    average = jnp.mean(values, axis=-1, keepdims=True)
    centered = values - average
    variance = jnp.mean(centered * centered, axis=-1, keepdims=True)
    return centered * lax.rsqrt(variance + EPSILON) * gain_row


def iota(shape, dim):
    return lax.broadcasted_iota(jnp.int32, shape, dim)


def fold(block):
    extra = block[TILE:]
    half = block.shape[1] // 2
    return jnp.concatenate([block[:TILE], jnp.concatenate([extra[:, :half], extra[:, half:]], axis=0)], axis=1)


def mm(a, b):
    return jnp.dot(a, b, preferred_element_type=F32)


def mm_t(a, b):
    return lax.dot_general(a, b, (((1,), (1,)), ((), ())), preferred_element_type=F32)


def kernel(
    n_img, n_txt,
    img_hbm, prompt_hbm, ids_hbm, valid_hbm, igain_hbm, pgain_hbm,
    wq_hbm, wk_hbm, wvi_hbm, wvp_hbm, woi_hbm, wop_hbm, iscale_hbm, pscale_hbm,
    out_img, out_prompt, out_cat,
    img_ref, prompt_ref, ids_ref, valid_ref, igain_ref, pgain_ref, iscale_ref, pscale_ref,
    wq, wk, wvi, wvp, woi, wop, xi, xp, meta, queries, keys, values_i, values_p, exp_c, exp_r,
    stat_r, stat_c, di_out, di_in, dp_out, dp_in, win, tally, cat,
    in_sem, w_sem, xi_s, xi_r, relay_s, xp_s, xp_r, meta_s, meta_r, sr_s, sr_r, sc_s, sc_r,
    di_s, di_r, dp_s, dp_r, win_s, win_r, tally_s, tally_r, cat_s, cat_r,
):
    my_img, my_txt = lax.axis_index("img"), lax.axis_index("txt")
    rows, width = img_ref.shape
    half = width // 2
    tokens = prompt_ref.shape[0]
    spare = tokens - TILE
    embed = wq.shape[1]
    heads = embed // HD
    n_rows = n_txt * rows
    n_cols = n_img * tokens
    cats = out_cat.shape[0]
    cat_lanes = tally.shape[2]

    inputs = (
        (prompt_hbm, prompt_ref), (pgain_hbm, pgain_ref), (valid_hbm, valid_ref), (ids_hbm, ids_ref),
        (img_hbm, img_ref), (igain_hbm, igain_ref), (iscale_hbm, iscale_ref), (pscale_hbm, pscale_ref),
    )
    fetches = [pltpu.make_async_copy(src, dst, in_sem.at[n]) for n, (src, dst) in enumerate(inputs)]
    weights = ((wq_hbm, wq), (wvi_hbm, wvi), (wk_hbm, wk), (wvp_hbm, wvp), (wop_hbm, wop), (woi_hbm, woi))
    loads = [pltpu.make_async_copy(src, dst, w_sem.at[n]) for n, (src, dst) in enumerate(weights)]
    for fetch in fetches:
        fetch.start()

    def others(axis, body):
        count, mine = (n_img, my_img) if axis == "img" else (n_txt, my_txt)
        if count <= 8:
            for step in sorted(range(1, count), key=lambda n: abs(2 * n - count)):
                body(lax.rem(mine + step, count))
        else:

            @pl.loop(1, count)
            def _(step):
                body(lax.rem(mine + step, count))

    def place(axis, p):
        return {"img": p, "txt": my_txt} if axis == "img" else {"img": my_img, "txt": p}

    barrier = pltpu.get_barrier_semaphore()
    for axis in ("img", "txt"):
        others(axis, lambda p: pl.semaphore_signal(barrier, inc=1, device_id=place(axis, p), device_id_type=MESH))
    for load in loads:
        load.start()

    def send(axis, src, dst, s, r):
        mine = my_img if axis == "img" else my_txt
        others(
            axis,
            lambda p: pltpu.make_async_remote_copy(
                src(p), dst.at[mine], s.at[0], r.at[0], device_id=place(axis, p), device_id_type=MESH
            ).start(),
        )

    def whole(buf, s, r):
        part = buf.at[pl.ds(0, buf.shape[0] - 1)]
        return pltpu.make_async_remote_copy(
            part, part, s.at[0], r.at[0], device_id={"img": my_img, "txt": my_txt}, device_id_type=MESH
        )

    for fetch in fetches[:4]:
        fetch.wait()
    xp[my_img] = fold(normalize(prompt_ref[...], pgain_ref[...].reshape(1, width))).astype(BF16)

    valid_row = valid_ref[...].reshape(1, tokens)
    ids_row = ids_ref[...].reshape(1, tokens)
    first_id = ids_row[:, 0:1]
    members = jnp.logical_and(ids_row - first_id == iota((WINDOW, tokens), 0), valid_row > 0).astype(F32)
    counts = jnp.sum(members, axis=1, keepdims=True).astype(jnp.int32)
    lane = iota((WINDOW, 128), 1) - (my_img % 8) * TILE
    slot = iota((WINDOW, 128), 0)
    own_lane = jnp.logical_and(jnp.logical_and(lane >= 0, lane < TILE), lane % WINDOW == slot)
    numbers = jnp.sum(jnp.where(own_lane, counts * COUNT_BASE + first_id + slot, 0), axis=0, keepdims=True)
    diagonal = iota((tokens, tokens), 0) == iota((tokens, tokens), 1)
    valid_col = jnp.sum(jnp.where(diagonal, jnp.broadcast_to(valid_row, (tokens, tokens)), 0), axis=1, keepdims=True)

    def marks(at, first, count):
        here = at + iota((count, 128), 0) == iota((count, 128), 1)
        return jnp.sum(jnp.where(here, valid_col[first : first + count], 0), axis=0, keepdims=True)

    meta[my_img] = jnp.concatenate(
        [numbers, marks((my_img % 8) * TILE, 0, TILE), marks((my_img % (128 // spare)) * spare, TILE, spare)], axis=1
    )

    fetches[4].wait()
    fetches[5].wait()
    xi[my_txt] = normalize(img_ref[...], igain_ref[...].reshape(1, width)).astype(BF16)

    pl.semaphore_wait(barrier, n_img - 1 + n_txt - 1)

    def image_copy(p, at):
        return pltpu.make_async_remote_copy(
            xi.at[at], xi.at[at], xi_s.at[p], xi_r.at[at], device_id=place("txt", p), device_id_type=MESH
        )

    mate = my_txt + 1 - 2 * (my_txt % 2)
    far = [lax.rem(my_txt + 2 * step, n_txt) for step in range(1, n_txt // 2)]
    send("img", lambda p: xp.at[my_img], xp, xp_s, xp_r)
    for p in far:
        image_copy(p, my_txt).start()
    image_copy(mate, my_txt).start()
    send("img", lambda p: meta.at[my_img], meta, meta_s, meta_r)

    def image_rows(p):
        return pl.ds(pl.multiple_of(p * rows, rows), rows)

    def project_queries(p):
        queries[image_rows(p), :] = (mm(xi[p], wq[...]) * (HD ** -0.5)).astype(BF16)

    def project_values(p):
        values_i[image_rows(p), :] = mm(xi[p], wvi[...]).astype(BF16)

    def relay(p):
        return pltpu.make_async_remote_copy(
            xi.at[p], xi.at[p], relay_s.at[p], xi_r.at[p], device_id=place("txt", mate), device_id_type=MESH
        )

    loads[0].wait()
    project_queries(my_txt)
    for p in far:
        image_copy(p, p).wait_recv()
        relay(p).start()
    loads[1].wait()
    project_values(my_txt)
    image_copy(mate, mate).wait_recv()
    project_queries(mate)
    project_values(mate)
    for p in far:
        project_queries(p)
        project_values(p)

    whole(xp, xp_s, xp_r).wait_recv()
    tall = xp[:, :, :width].reshape(n_img * TILE, width)
    short = xp[:, :, width:].astype(F32)
    short = jnp.concatenate([short[:, :spare], short[:, spare:]], axis=2).reshape(n_img * spare, width)
    x_prompt = jnp.concatenate([tall, short.astype(BF16)], axis=0)
    loads[2].wait()
    keys[...] = mm(x_prompt, wk[...]).astype(BF16)
    beyond = [p + 1 - 2 * (p % 2) for p in far]
    for p in beyond:
        image_copy(p, p).wait_recv()
        project_queries(p)

    def over_heads(body, stats):
        if n_cols <= 512:
            for h in range(heads):
                stats = body(h, stats)
            return stats
        return lax.fori_loop(0, heads, body, stats)

    def head(h):
        return pl.ds(h * HD, HD) if isinstance(h, int) else pl.ds(pl.multiple_of(h * HD, HD), HD)

    def put(h, stats, top, total):
        at = iota(stats.shape, 1)
        return jnp.where(at == h, top, jnp.where(at == heads + h, total, stats))

    def column_head(h, stats):
        scores = mm_t(keys[:, head(h)], queries[:, head(h)])
        top = jnp.max(scores, axis=1, keepdims=True)
        exps = jnp.exp(scores - top)
        exp_c[h] = exps.astype(BF16)
        return put(h, stats, top, jnp.sum(exps, axis=1, keepdims=True))

    def row_head(h, stats):
        scores = jnp.where(mask, mm_t(queries[:, head(h)], keys[:, head(h)]), MASKED)
        top = jnp.maximum(jnp.max(scores, axis=1, keepdims=True), FLOOR)
        exps = jnp.exp(scores - top)
        exp_r[h] = exps.astype(BF16)
        return put(h, stats, top, jnp.sum(exps, axis=1, keepdims=True))

    stats = over_heads(column_head, jnp.zeros((n_cols, 128), F32))
    stat_c[my_img] = stats.T[: 2 * heads]
    send("img", lambda p: stat_c.at[my_img], stat_c, sc_s, sc_r)
    loads[3].wait()
    for p in beyond:
        project_values(p)
    values_p[...] = mm(x_prompt, wvp[...]).astype(BF16)
    whole(meta, meta_s, meta_r).wait_recv()
    per = 128 // spare
    tall_marks = [jnp.sum(meta[g * 8 : g * 8 + 8, :, 128:256], axis=0) for g in range(n_img // 8)]
    short_marks = [jnp.sum(meta[g : min(g + per, n_img), :, 256:], axis=0) for g in range(0, n_img, per)]
    mask = jnp.concatenate(tall_marks + short_marks, axis=1)[:, :n_cols] > 0
    stats = over_heads(row_head, jnp.zeros((n_rows, 128), F32))
    stat_r[my_txt] = stats.T[: 2 * heads]
    send("txt", lambda p: stat_r.at[my_txt], stat_r, sr_s, sr_r)

    def factor(buf, mine):
        tops, sums = buf[:, :heads, :], buf[:, heads:, :]
        top = jnp.max(tops, axis=0)
        total = jnp.sum(sums * jnp.exp(tops - top[None]), axis=0)
        own = jnp.exp(buf[mine][:heads] - top) / total
        return jnp.concatenate([own, jnp.zeros((128 - heads, own.shape[1]), F32)], axis=0).T

    def numerators(exps, values):
        return [mm(exps[h], values[:, head(h)]) for h in range(heads)]

    def update(numers, scale, out_weight):
        delta = 0.0
        for h in range(heads):
            delta += mm((numers[h] * scale[:, h : h + 1]).astype(BF16), out_weight[head(h), :])
        return delta

    numers_p = numerators(exp_c, values_i)
    numers_i = numerators(exp_r, values_p)
    loads[4].wait()
    whole(stat_c, sc_s, sc_r).wait_recv()
    delta = update(numers_p, factor(stat_c, my_img), wop)
    tall = delta[: n_img * TILE].reshape(n_img, TILE, width)
    short = delta[n_img * TILE :].reshape(n_img, spare, width)
    short = jnp.concatenate([short[:, :, :half], short[:, :, half:]], axis=1)
    dp_out[...] = jnp.concatenate([tall, short], axis=2).astype(BF16)
    dp_in[my_img] = dp_out[my_img]
    send("img", lambda p: dp_out.at[p], dp_in, dp_s, dp_r)

    packed = jnp.concatenate([jnp.sum(meta[g * 8 : g * 8 + 8, :, :128], axis=0) for g in range(n_img // 8)], axis=1)
    key = jnp.broadcast_to(packed % COUNT_BASE, (cat_lanes, n_img * 16)) == iota((cat_lanes, n_img * 16), 0)
    low = iota((cat_lanes, n_img * 16), 1) % 16 < WINDOW
    pick_lo = jnp.where(jnp.logical_and(key, low), 1.0, 0.0).astype(BF16)
    pick_hi = jnp.where(jnp.logical_and(key, jnp.logical_not(low)), 1.0, 0.0).astype(BF16)
    numbers = jnp.broadcast_to((packed // COUNT_BASE).astype(F32), (8, n_img * 16)).astype(BF16)
    tally[my_txt] = mm_t(numbers, pick_lo)
    send("txt", lambda p: tally.at[my_txt], tally, tally_s, tally_r)

    loads[5].wait()
    whole(stat_r, sr_s, sr_r).wait_recv()
    di_out[...] = update(numers_i, factor(stat_r, my_txt), woi).astype(BF16).reshape(di_out.shape)
    di_in[my_txt] = di_out[my_txt]
    send("txt", lambda p: di_out.at[p], di_in, di_s, di_r)

    whole(dp_in, dp_s, dp_r).wait_recv()
    total = jnp.sum(dp_in[...].astype(F32), axis=0)
    short = jnp.concatenate([total[:spare, width:], total[spare:, width:]], axis=1)
    prompt_delta = jnp.concatenate([total[:, :width], short], axis=0)
    fetches[6].wait()
    fetches[7].wait()
    joined = prompt_ref[...].astype(F32) + pscale_ref[...].reshape(1, width) * prompt_delta
    sums = jnp.dot(members, joined, precision=lax.Precision.HIGHEST, preferred_element_type=F32)
    win[my_img] = jnp.concatenate([sums[:, :half], sums[:, half:]], axis=0).astype(BF16)
    send("img", lambda p: win.at[my_img], win, win_s, win_r)
    out_prompt[...] = joined.astype(BF16)

    whole(di_in, di_s, di_r).wait_recv()
    image_delta = jnp.sum(di_in[...].astype(F32), axis=0)
    out_img[...] = (img_ref[...].astype(F32) + iscale_ref[...].reshape(1, width) * image_delta).astype(BF16)

    whole(win, win_s, win_r).wait_recv()
    windows = win[...].reshape(n_img * 16, half)
    block = jnp.concatenate([mm(pick_lo[:cats], windows), mm(pick_hi[:cats], windows)], axis=1)
    cat[my_txt] = block.astype(BF16)
    send("txt", lambda p: cat.at[my_txt], cat, cat_s, cat_r)

    whole(tally, tally_s, tally_r).wait_recv()
    tally_row = jnp.sum(tally[...], axis=0)[0:1]
    on_diagonal = iota((cats, cat_lanes), 0) == iota((cats, cat_lanes), 1)
    tally_col = jnp.sum(jnp.where(on_diagonal, tally_row, 0.0), axis=1, keepdims=True)
    whole(cat, cat_s, cat_r).wait_recv()
    out_cat[...] = jnp.sum(cat[...].astype(F32), axis=0) / tally_col

    for p in far:
        image_copy(p, my_txt).wait_send()
        relay(p).wait_send()
    image_copy(mate, my_txt).wait_send()
    for buf, s, r in (
        (xp, xp_s, xp_r), (meta, meta_s, meta_r), (stat_c, sc_s, sc_r), (stat_r, sr_s, sr_r), (dp_in, dp_s, dp_r),
        (tally, tally_s, tally_r), (di_in, di_s, di_r), (win, win_s, win_r), (cat, cat_s, cat_r),
    ):
        whole(buf, s, r).wait_send()


def keep(*refs):
    count = len(refs) // 2
    for n in range(count):
        refs[count + n][...] = refs[n][...]


def on_device(n_img, n_txt, image_tokens, prompt_tokens, *rest):
    rows, width = image_tokens.shape
    tokens = prompt_tokens.shape[0]
    embed = rest[4].shape[1]
    heads = embed // HD
    n_rows, n_cols = n_txt * rows, n_img * tokens
    folded = width + width // 2
    cats = n_img * n_txt * tokens // 16
    cat_lanes = (cats + 127) // 128 * 128
    vmem, hbm = pl.BlockSpec(memory_space=pltpu.VMEM), pl.BlockSpec(memory_space=pl.ANY)
    dma = pltpu.SemaphoreType.DMA
    one = (dma((1,)), dma((1,)))
    outs = (
        jax.ShapeDtypeStruct((rows, width), BF16),
        jax.ShapeDtypeStruct((tokens, width), BF16),
        jax.ShapeDtypeStruct((cats, width), F32),
    )
    results = pl.pallas_call(
        functools.partial(kernel, n_img, n_txt),
        out_shape=tuple(pltpu.VMEM(out.shape, out.dtype) for out in outs),
        in_specs=[hbm] * 14,
        out_specs=(vmem, vmem, vmem),
        scratch_shapes=[pltpu.VMEM(x.shape, x.dtype) for x in (image_tokens, prompt_tokens, *rest[:4], *rest[10:])]
        + [pltpu.VMEM((width, embed), BF16)] * 4
        + [pltpu.VMEM((embed, width), BF16)] * 2
        + [
            pltpu.VMEM((n_txt, rows, width), BF16),
            pltpu.VMEM((n_img, TILE, folded), BF16),
            pltpu.VMEM((n_img, 1, 384), jnp.int32),
            pltpu.VMEM((n_rows, embed), BF16),
            pltpu.VMEM((n_cols, embed), BF16),
            pltpu.VMEM((n_rows, embed), BF16),
            pltpu.VMEM((n_cols, embed), BF16),
            pltpu.VMEM((heads, n_cols, n_rows), BF16),
            pltpu.VMEM((heads, n_rows, n_cols), BF16),
            pltpu.VMEM((n_txt, 2 * heads, n_rows), F32),
            pltpu.VMEM((n_img, 2 * heads, n_cols), F32),
            pltpu.VMEM((n_txt, rows, width), BF16),
            pltpu.VMEM((n_txt, rows, width), BF16),
            pltpu.VMEM((n_img, TILE, folded), BF16),
            pltpu.VMEM((n_img, TILE, folded), BF16),
            pltpu.VMEM((n_img, 16, width // 2), BF16),
            pltpu.VMEM((n_txt, 8, cat_lanes), F32),
            pltpu.VMEM((n_txt, cats, width), BF16),
            dma((8,)),
            dma((6,)),
            dma((n_txt,)),
            dma((n_txt,)),
            dma((n_txt,)),
            *one, *one, *one, *one, *one, *one, *one, *one, *one,
        ],
        compiler_params=pltpu.CompilerParams(
            collective_id=0, has_side_effects=True, vmem_limit_bytes=56 * 2**20
        ),
        name="joining_layer",
    )(image_tokens, prompt_tokens, *rest)
    return pl.pallas_call(
        keep,
        out_shape=outs,
        in_specs=[vmem] * len(outs),
        out_specs=(vmem,) * len(outs),
        compiler_params=pltpu.CompilerParams(vmem_limit_bytes=2**20),
        name="keep",
    )(*results)


def solution(mesh):
    return jax.shard_map(
        functools.partial(on_device, mesh.shape["img"], mesh.shape["txt"]),
        mesh=mesh,
        in_specs=(
            P(("img", "txt"), None),
            P(("txt", "img"), None),
            P(("txt", "img")),
            P(("txt", "img")),
        )
        + (P(),) * 10,
        out_specs=(P(("img", "txt"), None), P(("txt", "img"), None), P()),
        check_vma=False,
    )
```

```python
import functools

import jax
import jax.numpy as jnp
from jax import lax
from jax.experimental import pallas as pl
from jax.experimental.pallas import tpu as pltpu
from jax.sharding import PartitionSpec as P

HD = 256
EPSILON = 1e-05
MASKED = -1e30
FLOOR = -1e29
WINDOW = 8
COUNT_BASE = 4096
TILE = 16
MESH = pl.DeviceIdType.MESH
F32 = jnp.float32
BF16 = jnp.bfloat16


def normalize(tokens_in, gain_row):
    values = tokens_in.astype(F32)
    average = jnp.mean(values, axis=-1, keepdims=True)
    centered = values - average
    variance = jnp.mean(centered * centered, axis=-1, keepdims=True)
    return centered * lax.rsqrt(variance + EPSILON) * gain_row


def iota(shape, dim):
    return lax.broadcasted_iota(jnp.int32, shape, dim)


def fold(block):
    extra = block[TILE:]
    half = block.shape[1] // 2
    return jnp.concatenate([block[:TILE], jnp.concatenate([extra[:, :half], extra[:, half:]], axis=0)], axis=1)


def mm(a, b):
    return jnp.dot(a, b, preferred_element_type=F32)


def mm_t(a, b):
    return lax.dot_general(a, b, (((1,), (1,)), ((), ())), preferred_element_type=F32)


def kernel(
    n_img, n_txt,
    img_hbm, prompt_hbm, ids_hbm, valid_hbm, igain_hbm, pgain_hbm,
    wq_hbm, wk_hbm, wvi_hbm, wvp_hbm, woi_hbm, wop_hbm, iscale_hbm, pscale_hbm,
    out_img, out_prompt, out_cat,
    img_ref, prompt_ref, ids_ref, valid_ref, igain_ref, pgain_ref, iscale_ref, pscale_ref,
    wq, wk, wvi, wvp, woi, wop, xi, xp, meta, queries, keys, values_i, values_p, exp_c, exp_r,
    stat_r, stat_c, di_out, di_in, dp_out, dp_in, win, tally, cat,
    in_sem, w_sem, xi_s, xi_r, relay_s, xp_s, xp_r, meta_s, meta_r, sr_s, sr_r, sc_s, sc_r,
    di_s, di_r, dp_s, dp_r, win_s, win_r, tally_s, tally_r, cat_s, cat_r,
):
    my_img, my_txt = lax.axis_index("img"), lax.axis_index("txt")
    rows, width = img_ref.shape
    half = width // 2
    tokens = prompt_ref.shape[0]
    spare = tokens - TILE
    embed = wq.shape[1]
    heads = embed // HD
    n_rows = n_txt * rows
    n_cols = n_img * tokens
    cats = out_cat.shape[0]
    cat_lanes = tally.shape[2]

    inputs = (
        (prompt_hbm, prompt_ref), (pgain_hbm, pgain_ref), (valid_hbm, valid_ref), (ids_hbm, ids_ref),
        (img_hbm, img_ref), (igain_hbm, igain_ref), (iscale_hbm, iscale_ref), (pscale_hbm, pscale_ref),
    )
    fetches = [pltpu.make_async_copy(src, dst, in_sem.at[n]) for n, (src, dst) in enumerate(inputs)]
    weights = ((wq_hbm, wq), (wvi_hbm, wvi), (wk_hbm, wk), (wvp_hbm, wvp), (wop_hbm, wop), (woi_hbm, woi))
    loads = [pltpu.make_async_copy(src, dst, w_sem.at[n]) for n, (src, dst) in enumerate(weights)]
    for fetch in fetches:
        fetch.start()

    def others(axis, body):
        count, mine = (n_img, my_img) if axis == "img" else (n_txt, my_txt)
        if count <= 8:
            for step in sorted(range(1, count), key=lambda n: abs(2 * n - count)):
                body(lax.rem(mine + step, count))
        else:

            @pl.loop(1, count)
            def _(step):
                body(lax.rem(mine + step, count))

    def place(axis, p):
        return {"img": p, "txt": my_txt} if axis == "img" else {"img": my_img, "txt": p}

    barrier = pltpu.get_barrier_semaphore()
    for axis in ("img", "txt"):
        others(axis, lambda p: pl.semaphore_signal(barrier, inc=1, device_id=place(axis, p), device_id_type=MESH))
    for load in loads:
        load.start()

    def send(axis, src, dst, s, r):
        mine = my_img if axis == "img" else my_txt
        others(
            axis,
            lambda p: pltpu.make_async_remote_copy(
                src(p), dst.at[mine], s.at[0], r.at[0], device_id=place(axis, p), device_id_type=MESH
            ).start(),
        )

    def whole(buf, s, r):
        part = buf.at[pl.ds(0, buf.shape[0] - 1)]
        return pltpu.make_async_remote_copy(
            part, part, s.at[0], r.at[0], device_id={"img": my_img, "txt": my_txt}, device_id_type=MESH
        )

    for fetch in fetches[:4]:
        fetch.wait()
    xp[my_img] = fold(normalize(prompt_ref[...], pgain_ref[...].reshape(1, width))).astype(BF16)

    valid_row = valid_ref[...].reshape(1, tokens)
    ids_row = ids_ref[...].reshape(1, tokens)
    first_id = ids_row[:, 0:1]
    members = jnp.logical_and(ids_row - first_id == iota((WINDOW, tokens), 0), valid_row > 0).astype(F32)
    counts = jnp.sum(members, axis=1, keepdims=True).astype(jnp.int32)
    lane = iota((WINDOW, 128), 1) - (my_img % 8) * TILE
    slot = iota((WINDOW, 128), 0)
    own_lane = jnp.logical_and(jnp.logical_and(lane >= 0, lane < TILE), lane % WINDOW == slot)
    numbers = jnp.sum(jnp.where(own_lane, counts * COUNT_BASE + first_id + slot, 0), axis=0, keepdims=True)
    diagonal = iota((tokens, tokens), 0) == iota((tokens, tokens), 1)
    valid_col = jnp.sum(jnp.where(diagonal, jnp.broadcast_to(valid_row, (tokens, tokens)), 0), axis=1, keepdims=True)

    def marks(at, first, count):
        here = at + iota((count, 128), 0) == iota((count, 128), 1)
        return jnp.sum(jnp.where(here, valid_col[first : first + count], 0), axis=0, keepdims=True)

    meta[my_img] = jnp.concatenate(
        [numbers, marks((my_img % 8) * TILE, 0, TILE), marks((my_img % (128 // spare)) * spare, TILE, spare)], axis=1
    )

    fetches[4].wait()
    fetches[5].wait()
    xi[my_txt] = normalize(img_ref[...], igain_ref[...].reshape(1, width)).astype(BF16)

    pl.semaphore_wait(barrier, n_img - 1 + n_txt - 1)

    def image_copy(p, at):
        return pltpu.make_async_remote_copy(
            xi.at[at], xi.at[at], xi_s.at[p], xi_r.at[at], device_id=place("txt", p), device_id_type=MESH
        )

    mate = my_txt + 1 - 2 * (my_txt % 2)
    far = [lax.rem(my_txt + 2 * step, n_txt) for step in range(1, n_txt // 2)]
    send("img", lambda p: xp.at[my_img], xp, xp_s, xp_r)
    for p in far:
        image_copy(p, my_txt).start()
    image_copy(mate, my_txt).start()
    send("img", lambda p: meta.at[my_img], meta, meta_s, meta_r)

    def image_rows(p):
        return pl.ds(pl.multiple_of(p * rows, rows), rows)

    def project_queries(p):
        queries[image_rows(p), :] = (mm(xi[p], wq[...]) * (HD ** -0.5)).astype(BF16)

    def project_values(p):
        values_i[image_rows(p), :] = mm(xi[p], wvi[...]).astype(BF16)

    def relay(p):
        return pltpu.make_async_remote_copy(
            xi.at[p], xi.at[p], relay_s.at[p], xi_r.at[p], device_id=place("txt", mate), device_id_type=MESH
        )

    loads[0].wait()
    project_queries(my_txt)
    for p in far:
        image_copy(p, p).wait_recv()
        relay(p).start()
    loads[1].wait()
    project_values(my_txt)
    image_copy(mate, mate).wait_recv()
    project_queries(mate)
    project_values(mate)
    for p in far:
        project_queries(p)
        project_values(p)

    whole(xp, xp_s, xp_r).wait_recv()
    tall = xp[:, :, :width].reshape(n_img * TILE, width)
    short = xp[:, :, width:].astype(F32)
    short = jnp.concatenate([short[:, :spare], short[:, spare:]], axis=2).reshape(n_img * spare, width)
    x_prompt = jnp.concatenate([tall, short.astype(BF16)], axis=0)
    loads[2].wait()
    keys[...] = mm(x_prompt, wk[...]).astype(BF16)
    beyond = [p + 1 - 2 * (p % 2) for p in far]
    for p in beyond:
        image_copy(p, p).wait_recv()
        project_queries(p)

    def over_heads(body, stats):
        if n_cols <= 512:
            for h in range(heads):
                stats = body(h, stats)
            return stats
        return lax.fori_loop(0, heads, body, stats)

    def head(h):
        return pl.ds(h * HD, HD) if isinstance(h, int) else pl.ds(pl.multiple_of(h * HD, HD), HD)

    def put(h, stats, top, total):
        at = iota(stats.shape, 1)
        return jnp.where(at == h, top, jnp.where(at == heads + h, total, stats))

    def column_head(h, stats):
        scores = mm_t(keys[:, head(h)], queries[:, head(h)])
        top = jnp.max(scores, axis=1, keepdims=True)
        exps = jnp.exp(scores - top)
        exp_c[h] = exps.astype(BF16)
        return put(h, stats, top, jnp.sum(exps, axis=1, keepdims=True))

    def row_head(h, stats):
        scores = jnp.where(mask, mm_t(queries[:, head(h)], keys[:, head(h)]), MASKED)
        top = jnp.maximum(jnp.max(scores, axis=1, keepdims=True), FLOOR)
        exps = jnp.exp(scores - top)
        exp_r[h] = exps.astype(BF16)
        return put(h, stats, top, jnp.sum(exps, axis=1, keepdims=True))

    stats = over_heads(column_head, jnp.zeros((n_cols, 128), F32))
    stat_c[my_img] = stats.T[: 2 * heads]
    send("img", lambda p: stat_c.at[my_img], stat_c, sc_s, sc_r)
    def factor(buf, mine):
        tops, sums = buf[:, :heads, :], buf[:, heads:, :]
        top = jnp.max(tops, axis=0)
        total = jnp.sum(sums * jnp.exp(tops - top[None]), axis=0)
        own = jnp.exp(buf[mine][:heads] - top) / total
        return jnp.concatenate([own, jnp.zeros((128 - heads, own.shape[1]), F32)], axis=0).T

    def numerators(exps, values):
        return [mm(exps[h], values[:, head(h)]) for h in range(heads)]

    def update(numers, scale, out_weight):
        delta = 0.0
        for h in range(heads):
            delta += mm((numers[h] * scale[:, h : h + 1]).astype(BF16), out_weight[head(h), :])
        return delta

    for p in beyond:
        project_values(p)
    numers_p = numerators(exp_c, values_i)
    loads[3].wait()
    values_p[...] = mm(x_prompt, wvp[...]).astype(BF16)
    whole(meta, meta_s, meta_r).wait_recv()
    per = 128 // spare
    tall_marks = [jnp.sum(meta[g * 8 : g * 8 + 8, :, 128:256], axis=0) for g in range(n_img // 8)]
    short_marks = [jnp.sum(meta[g : min(g + per, n_img), :, 256:], axis=0) for g in range(0, n_img, per)]
    mask = jnp.concatenate(tall_marks + short_marks, axis=1)[:, :n_cols] > 0
    loads[4].wait()
    whole(stat_c, sc_s, sc_r).wait_recv()
    delta = update(numers_p, factor(stat_c, my_img), wop)
    tall = delta[: n_img * TILE].reshape(n_img, TILE, width)
    short = delta[n_img * TILE :].reshape(n_img, spare, width)
    short = jnp.concatenate([short[:, :, :half], short[:, :, half:]], axis=1)
    dp_out[...] = jnp.concatenate([tall, short], axis=2).astype(BF16)
    dp_in[my_img] = dp_out[my_img]
    send("img", lambda p: dp_out.at[p], dp_in, dp_s, dp_r)

    stats = over_heads(row_head, jnp.zeros((n_rows, 128), F32))
    stat_r[my_txt] = stats.T[: 2 * heads]
    send("txt", lambda p: stat_r.at[my_txt], stat_r, sr_s, sr_r)

    packed = jnp.concatenate([jnp.sum(meta[g * 8 : g * 8 + 8, :, :128], axis=0) for g in range(n_img // 8)], axis=1)
    key = jnp.broadcast_to(packed % COUNT_BASE, (cat_lanes, n_img * 16)) == iota((cat_lanes, n_img * 16), 0)
    low = iota((cat_lanes, n_img * 16), 1) % 16 < WINDOW
    pick_lo = jnp.where(jnp.logical_and(key, low), 1.0, 0.0).astype(BF16)
    pick_hi = jnp.where(jnp.logical_and(key, jnp.logical_not(low)), 1.0, 0.0).astype(BF16)
    numbers = jnp.broadcast_to((packed // COUNT_BASE).astype(F32), (8, n_img * 16)).astype(BF16)
    tally[my_txt] = mm_t(numbers, pick_lo)
    send("txt", lambda p: tally.at[my_txt], tally, tally_s, tally_r)

    numers_i = numerators(exp_r, values_p)

    whole(dp_in, dp_s, dp_r).wait_recv()
    total = jnp.sum(dp_in[...].astype(F32), axis=0)
    short = jnp.concatenate([total[:spare, width:], total[spare:, width:]], axis=1)
    prompt_delta = jnp.concatenate([total[:, :width], short], axis=0)
    fetches[6].wait()
    fetches[7].wait()
    joined = prompt_ref[...].astype(F32) + pscale_ref[...].reshape(1, width) * prompt_delta
    sums = jnp.dot(members, joined, precision=lax.Precision.HIGHEST, preferred_element_type=F32)
    win[my_img] = jnp.concatenate([sums[:, :half], sums[:, half:]], axis=0).astype(BF16)
    send("img", lambda p: win.at[my_img], win, win_s, win_r)
    out_prompt[...] = joined.astype(BF16)

    loads[5].wait()
    whole(stat_r, sr_s, sr_r).wait_recv()
    di_out[...] = update(numers_i, factor(stat_r, my_txt), woi).astype(BF16).reshape(di_out.shape)
    di_in[my_txt] = di_out[my_txt]
    send("txt", lambda p: di_out.at[p], di_in, di_s, di_r)

    whole(win, win_s, win_r).wait_recv()
    windows = win[...].reshape(n_img * 16, half)
    block = jnp.concatenate([mm(pick_lo[:cats], windows), mm(pick_hi[:cats], windows)], axis=1)
    cat[my_txt] = block.astype(BF16)
    send("txt", lambda p: cat.at[my_txt], cat, cat_s, cat_r)

    whole(di_in, di_s, di_r).wait_recv()
    image_delta = jnp.sum(di_in[...].astype(F32), axis=0)
    out_img[...] = (img_ref[...].astype(F32) + iscale_ref[...].reshape(1, width) * image_delta).astype(BF16)

    whole(tally, tally_s, tally_r).wait_recv()
    tally_row = jnp.sum(tally[...], axis=0)[0:1]
    on_diagonal = iota((cats, cat_lanes), 0) == iota((cats, cat_lanes), 1)
    tally_col = jnp.sum(jnp.where(on_diagonal, tally_row, 0.0), axis=1, keepdims=True)
    whole(cat, cat_s, cat_r).wait_recv()
    out_cat[...] = jnp.sum(cat[...].astype(F32), axis=0) / tally_col

    for p in far:
        image_copy(p, my_txt).wait_send()
        relay(p).wait_send()
    image_copy(mate, my_txt).wait_send()
    for buf, s, r in (
        (xp, xp_s, xp_r), (meta, meta_s, meta_r), (stat_c, sc_s, sc_r), (stat_r, sr_s, sr_r), (dp_in, dp_s, dp_r),
        (tally, tally_s, tally_r), (di_in, di_s, di_r), (win, win_s, win_r), (cat, cat_s, cat_r),
    ):
        whole(buf, s, r).wait_send()


def keep(*refs):
    count = len(refs) // 2
    for n in range(count):
        refs[count + n][...] = refs[n][...]


def on_device(n_img, n_txt, image_tokens, prompt_tokens, *rest):
    rows, width = image_tokens.shape
    tokens = prompt_tokens.shape[0]
    embed = rest[4].shape[1]
    heads = embed // HD
    n_rows, n_cols = n_txt * rows, n_img * tokens
    folded = width + width // 2
    cats = n_img * n_txt * tokens // 16
    cat_lanes = (cats + 127) // 128 * 128
    vmem, hbm = pl.BlockSpec(memory_space=pltpu.VMEM), pl.BlockSpec(memory_space=pl.ANY)
    dma = pltpu.SemaphoreType.DMA
    one = (dma((1,)), dma((1,)))
    outs = (
        jax.ShapeDtypeStruct((rows, width), BF16),
        jax.ShapeDtypeStruct((tokens, width), BF16),
        jax.ShapeDtypeStruct((cats, width), F32),
    )
    results = pl.pallas_call(
        functools.partial(kernel, n_img, n_txt),
        out_shape=tuple(pltpu.VMEM(out.shape, out.dtype) for out in outs),
        in_specs=[hbm] * 14,
        out_specs=(vmem, vmem, vmem),
        scratch_shapes=[pltpu.VMEM(x.shape, x.dtype) for x in (image_tokens, prompt_tokens, *rest[:4], *rest[10:])]
        + [pltpu.VMEM((width, embed), BF16)] * 4
        + [pltpu.VMEM((embed, width), BF16)] * 2
        + [
            pltpu.VMEM((n_txt, rows, width), BF16),
            pltpu.VMEM((n_img, TILE, folded), BF16),
            pltpu.VMEM((n_img, 1, 384), jnp.int32),
            pltpu.VMEM((n_rows, embed), BF16),
            pltpu.VMEM((n_cols, embed), BF16),
            pltpu.VMEM((n_rows, embed), BF16),
            pltpu.VMEM((n_cols, embed), BF16),
            pltpu.VMEM((heads, n_cols, n_rows), BF16),
            pltpu.VMEM((heads, n_rows, n_cols), BF16),
            pltpu.VMEM((n_txt, 2 * heads, n_rows), F32),
            pltpu.VMEM((n_img, 2 * heads, n_cols), F32),
            pltpu.VMEM((n_txt, rows, width), BF16),
            pltpu.VMEM((n_txt, rows, width), BF16),
            pltpu.VMEM((n_img, TILE, folded), BF16),
            pltpu.VMEM((n_img, TILE, folded), BF16),
            pltpu.VMEM((n_img, 16, width // 2), BF16),
            pltpu.VMEM((n_txt, 8, cat_lanes), F32),
            pltpu.VMEM((n_txt, cats, width), BF16),
            dma((8,)),
            dma((6,)),
            dma((n_txt,)),
            dma((n_txt,)),
            dma((n_txt,)),
            *one, *one, *one, *one, *one, *one, *one, *one, *one,
        ],
        compiler_params=pltpu.CompilerParams(
            collective_id=0, has_side_effects=True, vmem_limit_bytes=56 * 2**20
        ),
        name="joining_layer",
    )(image_tokens, prompt_tokens, *rest)
    return pl.pallas_call(
        keep,
        out_shape=outs,
        in_specs=[vmem] * len(outs),
        out_specs=(vmem,) * len(outs),
        compiler_params=pltpu.CompilerParams(vmem_limit_bytes=2**20),
        name="keep",
    )(*results)


def solution(mesh):
    return jax.shard_map(
        functools.partial(on_device, mesh.shape["img"], mesh.shape["txt"]),
        mesh=mesh,
        in_specs=(
            P(("img", "txt"), None),
            P(("txt", "img"), None),
            P(("txt", "img")),
            P(("txt", "img")),
        )
        + (P(),) * 10,
        out_specs=(P(("img", "txt"), None), P(("txt", "img"), None), P()),
        check_vma=False,
    )
```

```python
import functools

import jax
import jax.numpy as jnp
from jax import lax
from jax.experimental import pallas as pl
from jax.experimental.pallas import tpu as pltpu
from jax.sharding import PartitionSpec as P

HD = 256
EPSILON = 1e-05
MASKED = -1e30
FLOOR = -1e29
WINDOW = 8
COUNT_BASE = 4096
TILE = 16
MESH = pl.DeviceIdType.MESH
F32 = jnp.float32
BF16 = jnp.bfloat16


def normalize(tokens_in, gain_row):
    values = tokens_in.astype(F32)
    average = jnp.mean(values, axis=-1, keepdims=True)
    centered = values - average
    variance = jnp.mean(centered * centered, axis=-1, keepdims=True)
    return centered * lax.rsqrt(variance + EPSILON) * gain_row


def iota(shape, dim):
    return lax.broadcasted_iota(jnp.int32, shape, dim)


def fold(block):
    extra = block[TILE:]
    half = block.shape[1] // 2
    return jnp.concatenate([block[:TILE], jnp.concatenate([extra[:, :half], extra[:, half:]], axis=0)], axis=1)


def mm(a, b):
    return jnp.dot(a, b, preferred_element_type=F32)


def mm_t(a, b):
    return lax.dot_general(a, b, (((1,), (1,)), ((), ())), preferred_element_type=F32)


def kernel(
    n_img, n_txt,
    img_hbm, prompt_hbm, ids_hbm, valid_hbm, igain_hbm, pgain_hbm,
    wq_hbm, wk_hbm, wvi_hbm, wvp_hbm, woi_hbm, wop_hbm, iscale_hbm, pscale_hbm,
    out_img, out_prompt, out_cat,
    img_ref, prompt_ref, ids_ref, valid_ref, igain_ref, pgain_ref, iscale_ref, pscale_ref,
    wq, wk, wvi, wvp, woi, wop, xi, xp, meta, queries, keys, values_i, values_p, exp_c,
    x_prompt, seen_c, seen_r, numer_p, numer_i, sum_p, sum_i,
    stat_r, stat_c, di_out, di_in, dp_out, dp_in, win, tally, cat,
    in_sem, w_sem, xi_s, xi_r, relay_s, xp_s, xp_r, meta_s, meta_r, sr_s, sr_r, sc_s, sc_r,
    di_s, di_r, dp_s, dp_r, win_s, win_r, tally_s, tally_r, cat_s, cat_r,
):
    my_img, my_txt = lax.axis_index("img"), lax.axis_index("txt")
    rows, width = img_ref.shape
    half = width // 2
    tokens = prompt_ref.shape[0]
    spare = tokens - TILE
    embed = wq.shape[1]
    heads = embed // HD
    n_rows = n_txt * rows
    n_cols = n_img * tokens
    cats = out_cat.shape[0]
    cat_lanes = tally.shape[2]

    inputs = (
        (prompt_hbm, prompt_ref), (pgain_hbm, pgain_ref), (valid_hbm, valid_ref), (ids_hbm, ids_ref),
        (img_hbm, img_ref), (igain_hbm, igain_ref), (iscale_hbm, iscale_ref), (pscale_hbm, pscale_ref),
    )
    fetches = [pltpu.make_async_copy(src, dst, in_sem.at[n]) for n, (src, dst) in enumerate(inputs)]
    weights = ((wq_hbm, wq), (wvi_hbm, wvi), (wk_hbm, wk), (wvp_hbm, wvp), (wop_hbm, wop), (woi_hbm, woi))
    loads = [pltpu.make_async_copy(src, dst, w_sem.at[n]) for n, (src, dst) in enumerate(weights)]
    for fetch in fetches:
        fetch.start()

    def others(axis, body):
        count, mine = (n_img, my_img) if axis == "img" else (n_txt, my_txt)
        if count <= 8:
            for step in sorted(range(1, count), key=lambda n: abs(2 * n - count)):
                body(lax.rem(mine + step, count))
        else:

            @pl.loop(1, count)
            def _(step):
                body(lax.rem(mine + step, count))

    def place(axis, p):
        return {"img": p, "txt": my_txt} if axis == "img" else {"img": my_img, "txt": p}

    barrier = pltpu.get_barrier_semaphore()
    for axis in ("img", "txt"):
        others(axis, lambda p: pl.semaphore_signal(barrier, inc=1, device_id=place(axis, p), device_id_type=MESH))
    for load in loads:
        load.start()

    def send(axis, src, dst, s, r):
        mine = my_img if axis == "img" else my_txt
        others(
            axis,
            lambda p: pltpu.make_async_remote_copy(
                src(p), dst.at[mine], s.at[0], r.at[0], device_id=place(axis, p), device_id_type=MESH
            ).start(),
        )

    def whole(buf, s, r):
        part = buf.at[pl.ds(0, buf.shape[0] - 1)]
        return pltpu.make_async_remote_copy(
            part, part, s.at[0], r.at[0], device_id={"img": my_img, "txt": my_txt}, device_id_type=MESH
        )

    for fetch in fetches[:4]:
        fetch.wait()
    xp[my_img] = fold(normalize(prompt_ref[...], pgain_ref[...].reshape(1, width))).astype(BF16)

    valid_row = valid_ref[...].reshape(1, tokens)
    ids_row = ids_ref[...].reshape(1, tokens)
    first_id = ids_row[:, 0:1]
    members = jnp.logical_and(ids_row - first_id == iota((WINDOW, tokens), 0), valid_row > 0).astype(F32)
    counts = jnp.sum(members, axis=1, keepdims=True).astype(jnp.int32)
    lane = iota((WINDOW, 128), 1) - (my_img % 8) * TILE
    slot = iota((WINDOW, 128), 0)
    own_lane = jnp.logical_and(jnp.logical_and(lane >= 0, lane < TILE), lane % WINDOW == slot)
    numbers = jnp.sum(jnp.where(own_lane, counts * COUNT_BASE + first_id + slot, 0), axis=0, keepdims=True)
    diagonal = iota((tokens, tokens), 0) == iota((tokens, tokens), 1)
    valid_col = jnp.sum(jnp.where(diagonal, jnp.broadcast_to(valid_row, (tokens, tokens)), 0), axis=1, keepdims=True)

    def marks(at, first, count):
        here = at + iota((count, 128), 0) == iota((count, 128), 1)
        return jnp.sum(jnp.where(here, valid_col[first : first + count], 0), axis=0, keepdims=True)

    meta[my_img] = jnp.concatenate(
        [numbers, marks((my_img % 8) * TILE, 0, TILE), marks((my_img % (128 // spare)) * spare, TILE, spare)], axis=1
    )

    fetches[4].wait()
    fetches[5].wait()
    xi[my_txt] = normalize(img_ref[...], igain_ref[...].reshape(1, width)).astype(BF16)

    seen_c[...] = jnp.zeros(seen_c.shape, F32)
    seen_r[...] = jnp.zeros(seen_r.shape, F32)
    pl.semaphore_wait(barrier, n_img - 1 + n_txt - 1)

    def image_copy(p, at):
        return pltpu.make_async_remote_copy(
            xi.at[at], xi.at[at], xi_s.at[p], xi_r.at[at], device_id=place("txt", p), device_id_type=MESH
        )

    mate = my_txt + 1 - 2 * (my_txt % 2)
    far = [lax.rem(my_txt + 2 * step, n_txt) for step in range(1, n_txt // 2)]
    send("img", lambda p: xp.at[my_img], xp, xp_s, xp_r)
    for p in far:
        image_copy(p, my_txt).start()
    image_copy(mate, my_txt).start()
    send("img", lambda p: meta.at[my_img], meta, meta_s, meta_r)

    def image_rows(p):
        return pl.ds(pl.multiple_of(p * rows, rows), rows)

    def head(h):
        return pl.ds(pl.multiple_of(h * HD, HD), HD)

    def project_queries(p):
        @pl.loop(0, heads)
        def _(h):
            queries[image_rows(p), head(h)] = (mm(xi[p], wq[:, head(h)]) * (HD ** -0.5)).astype(BF16)

    def project_values(p):
        @pl.loop(0, heads)
        def _(h):
            values_i[image_rows(p), head(h)] = mm(xi[p], wvi[:, head(h)]).astype(BF16)

    def relay(p):
        return pltpu.make_async_remote_copy(
            xi.at[p], xi.at[p], relay_s.at[p], xi_r.at[p], device_id=place("txt", mate), device_id_type=MESH
        )

    loads[0].wait()
    project_queries(my_txt)
    for p in far:
        image_copy(p, p).wait_recv()
        relay(p).start()
    loads[1].wait()
    project_values(my_txt)
    image_copy(mate, mate).wait_recv()
    project_queries(mate)
    project_values(mate)
    for p in far:
        project_queries(p)
        project_values(p)

    whole(xp, xp_s, xp_r).wait_recv()
    tall = xp[:, :, :width].reshape(n_img * TILE, width)
    short = xp[:, :, width:].astype(F32)
    short = jnp.concatenate([short[:, :spare], short[:, spare:]], axis=2).reshape(n_img * spare, width)
    x_prompt[...] = jnp.concatenate([tall, short.astype(BF16)], axis=0)
    loads[2].wait()

    @pl.loop(0, heads)
    def _(h):
        keys[:, head(h)] = mm(x_prompt[...], wk[:, head(h)]).astype(BF16)

    beyond = [p + 1 - 2 * (p % 2) for p in far]
    for p in beyond:
        image_copy(p, p).wait_recv()
        project_queries(p)

    def put(h, stats, top, total):
        at = iota(stats.shape, 1)
        stats[...] = jnp.where(at == h, top, jnp.where(at == heads + h, total, stats[...]))

    @pl.loop(0, heads)
    def _(h):
        scores = mm_t(keys[:, head(h)], queries[:, head(h)])
        top = jnp.max(scores, axis=1, keepdims=True)
        exps = jnp.exp(scores - top)
        exp_c[h] = exps.astype(BF16)
        put(h, seen_c, top, jnp.sum(exps, axis=1, keepdims=True))

    stat_c[my_img] = seen_c[...].T[: 2 * heads]
    send("img", lambda p: stat_c.at[my_img], stat_c, sc_s, sc_r)

    def factor(buf, mine):
        tops, sums = buf[:, :heads, :], buf[:, heads:, :]
        top = jnp.max(tops, axis=0)
        total = jnp.sum(sums * jnp.exp(tops - top[None]), axis=0)
        own = jnp.exp(buf[mine][:heads] - top) / total
        return jnp.concatenate([own, jnp.zeros((128 - heads, own.shape[1]), F32)], axis=0).T

    def update(numer, scale, out_weight, sums):
        sums[...] = jnp.zeros(sums.shape, F32)

        @pl.loop(0, heads)
        def _(h):
            own = jnp.sum(jnp.where(iota(scale.shape, 1) == h, scale, 0.0), axis=1, keepdims=True)
            sums[...] += mm((numer[h] * own).astype(BF16), out_weight[head(h), :])

        return sums[...]

    for p in beyond:
        project_values(p)

    @pl.loop(0, heads)
    def _(h):
        numer_p[h] = mm(exp_c[h], values_i[:, head(h)])

    loads[3].wait()

    @pl.loop(0, heads)
    def _(h):
        values_p[:, head(h)] = mm(x_prompt[...], wvp[:, head(h)]).astype(BF16)

    whole(meta, meta_s, meta_r).wait_recv()
    per = 128 // spare
    tall_marks = [jnp.sum(meta[g * 8 : g * 8 + 8, :, 128:256], axis=0) for g in range(n_img // 8)]
    short_marks = [jnp.sum(meta[g : min(g + per, n_img), :, 256:], axis=0) for g in range(0, n_img, per)]
    mask = jnp.concatenate(tall_marks + short_marks, axis=1)[:, :n_cols] > 0
    loads[4].wait()
    whole(stat_c, sc_s, sc_r).wait_recv()
    delta = update(numer_p, factor(stat_c, my_img), wop, sum_p)
    tall = delta[: n_img * TILE].reshape(n_img, TILE, width)
    short = delta[n_img * TILE :].reshape(n_img, spare, width)
    short = jnp.concatenate([short[:, :, :half], short[:, :, half:]], axis=1)
    dp_out[...] = jnp.concatenate([tall, short], axis=2).astype(BF16)
    dp_in[my_img] = dp_out[my_img]
    send("img", lambda p: dp_out.at[p], dp_in, dp_s, dp_r)

    @pl.loop(0, heads)
    def _(h):
        scores = jnp.where(mask, mm_t(queries[:, head(h)], keys[:, head(h)]), MASKED)
        top = jnp.maximum(jnp.max(scores, axis=1, keepdims=True), FLOOR)
        exps = jnp.exp(scores - top)
        put(h, seen_r, top, jnp.sum(exps, axis=1, keepdims=True))
        numer_i[h] = mm(exps.astype(BF16), values_p[:, head(h)])

    stat_r[my_txt] = seen_r[...].T[: 2 * heads]
    send("txt", lambda p: stat_r.at[my_txt], stat_r, sr_s, sr_r)

    packed = jnp.concatenate([jnp.sum(meta[g * 8 : g * 8 + 8, :, :128], axis=0) for g in range(n_img // 8)], axis=1)
    key = jnp.broadcast_to(packed % COUNT_BASE, (cat_lanes, n_img * 16)) == iota((cat_lanes, n_img * 16), 0)
    low = iota((cat_lanes, n_img * 16), 1) % 16 < WINDOW
    pick_lo = jnp.where(jnp.logical_and(key, low), 1.0, 0.0).astype(BF16)
    pick_hi = jnp.where(jnp.logical_and(key, jnp.logical_not(low)), 1.0, 0.0).astype(BF16)
    numbers = jnp.broadcast_to((packed // COUNT_BASE).astype(F32), (8, n_img * 16)).astype(BF16)
    tally[my_txt] = mm_t(numbers, pick_lo)
    send("txt", lambda p: tally.at[my_txt], tally, tally_s, tally_r)

    whole(dp_in, dp_s, dp_r).wait_recv()
    total = jnp.sum(dp_in[...].astype(F32), axis=0)
    short = jnp.concatenate([total[:spare, width:], total[spare:, width:]], axis=1)
    prompt_delta = jnp.concatenate([total[:, :width], short], axis=0)
    fetches[6].wait()
    fetches[7].wait()
    joined = prompt_ref[...].astype(F32) + pscale_ref[...].reshape(1, width) * prompt_delta
    sums = jnp.dot(members, joined, precision=lax.Precision.HIGHEST, preferred_element_type=F32)
    win[my_img] = jnp.concatenate([sums[:, :half], sums[:, half:]], axis=0).astype(BF16)
    send("img", lambda p: win.at[my_img], win, win_s, win_r)
    out_prompt[...] = joined.astype(BF16)

    loads[5].wait()
    whole(stat_r, sr_s, sr_r).wait_recv()
    di_out[...] = update(numer_i, factor(stat_r, my_txt), woi, sum_i).astype(BF16).reshape(di_out.shape)
    di_in[my_txt] = di_out[my_txt]
    send("txt", lambda p: di_out.at[p], di_in, di_s, di_r)

    whole(win, win_s, win_r).wait_recv()
    windows = win[...].reshape(n_img * 16, half)
    block = jnp.concatenate([mm(pick_lo[:cats], windows), mm(pick_hi[:cats], windows)], axis=1)
    cat[my_txt] = block.astype(BF16)
    send("txt", lambda p: cat.at[my_txt], cat, cat_s, cat_r)

    whole(di_in, di_s, di_r).wait_recv()
    image_delta = jnp.sum(di_in[...].astype(F32), axis=0)
    out_img[...] = (img_ref[...].astype(F32) + iscale_ref[...].reshape(1, width) * image_delta).astype(BF16)

    whole(tally, tally_s, tally_r).wait_recv()
    tally_row = jnp.sum(tally[...], axis=0)[0:1]
    on_diagonal = iota((cats, cat_lanes), 0) == iota((cats, cat_lanes), 1)
    tally_col = jnp.sum(jnp.where(on_diagonal, tally_row, 0.0), axis=1, keepdims=True)
    whole(cat, cat_s, cat_r).wait_recv()
    out_cat[...] = jnp.sum(cat[...].astype(F32), axis=0) / tally_col

    for p in far:
        image_copy(p, my_txt).wait_send()
        relay(p).wait_send()
    image_copy(mate, my_txt).wait_send()
    for buf, s, r in (
        (xp, xp_s, xp_r), (meta, meta_s, meta_r), (stat_c, sc_s, sc_r), (stat_r, sr_s, sr_r), (dp_in, dp_s, dp_r),
        (tally, tally_s, tally_r), (di_in, di_s, di_r), (win, win_s, win_r), (cat, cat_s, cat_r),
    ):
        whole(buf, s, r).wait_send()


def keep(*refs):
    count = len(refs) // 2
    for n in range(count):
        refs[count + n][...] = refs[n][...]


def on_device(n_img, n_txt, image_tokens, prompt_tokens, *rest):
    rows, width = image_tokens.shape
    tokens = prompt_tokens.shape[0]
    embed = rest[4].shape[1]
    heads = embed // HD
    n_rows, n_cols = n_txt * rows, n_img * tokens
    folded = width + width // 2
    cats = n_img * n_txt * tokens // 16
    cat_lanes = (cats + 127) // 128 * 128
    vmem, hbm = pl.BlockSpec(memory_space=pltpu.VMEM), pl.BlockSpec(memory_space=pl.ANY)
    dma = pltpu.SemaphoreType.DMA
    one = (dma((1,)), dma((1,)))
    outs = (
        jax.ShapeDtypeStruct((rows, width), BF16),
        jax.ShapeDtypeStruct((tokens, width), BF16),
        jax.ShapeDtypeStruct((cats, width), F32),
    )
    results = pl.pallas_call(
        functools.partial(kernel, n_img, n_txt),
        out_shape=tuple(pltpu.VMEM(out.shape, out.dtype) for out in outs),
        in_specs=[hbm] * 14,
        out_specs=(vmem, vmem, vmem),
        scratch_shapes=[pltpu.VMEM(x.shape, x.dtype) for x in (image_tokens, prompt_tokens, *rest[:4], *rest[10:])]
        + [pltpu.VMEM((width, embed), BF16)] * 4
        + [pltpu.VMEM((embed, width), BF16)] * 2
        + [
            pltpu.VMEM((n_txt, rows, width), BF16),
            pltpu.VMEM((n_img, TILE, folded), BF16),
            pltpu.VMEM((n_img, 1, 384), jnp.int32),
            pltpu.VMEM((n_rows, embed), BF16),
            pltpu.VMEM((n_cols, embed), BF16),
            pltpu.VMEM((n_rows, embed), BF16),
            pltpu.VMEM((n_cols, embed), BF16),
            pltpu.VMEM((heads, n_cols, n_rows), BF16),
            pltpu.VMEM((n_cols, width), BF16),
            pltpu.VMEM((n_cols, 128), F32),
            pltpu.VMEM((n_rows, 128), F32),
            pltpu.VMEM((heads, n_cols, HD), F32),
            pltpu.VMEM((heads, n_rows, HD), F32),
            pltpu.VMEM((n_cols, width), F32),
            pltpu.VMEM((n_rows, width), F32),
            pltpu.VMEM((n_txt, 2 * heads, n_rows), F32),
            pltpu.VMEM((n_img, 2 * heads, n_cols), F32),
            pltpu.VMEM((n_txt, rows, width), BF16),
            pltpu.VMEM((n_txt, rows, width), BF16),
            pltpu.VMEM((n_img, TILE, folded), BF16),
            pltpu.VMEM((n_img, TILE, folded), BF16),
            pltpu.VMEM((n_img, 16, width // 2), BF16),
            pltpu.VMEM((n_txt, 8, cat_lanes), F32),
            pltpu.VMEM((n_txt, cats, width), BF16),
            dma((8,)),
            dma((6,)),
            dma((n_txt,)),
            dma((n_txt,)),
            dma((n_txt,)),
            *one, *one, *one, *one, *one, *one, *one, *one, *one,
        ],
        compiler_params=pltpu.CompilerParams(
            collective_id=0, has_side_effects=True, vmem_limit_bytes=56 * 2**20
        ),
        name="joining_layer",
    )(image_tokens, prompt_tokens, *rest)
    return pl.pallas_call(
        keep,
        out_shape=outs,
        in_specs=[vmem] * len(outs),
        out_specs=(vmem,) * len(outs),
        compiler_params=pltpu.CompilerParams(vmem_limit_bytes=2**20),
        name="keep",
    )(*results)


def solution(mesh):
    return jax.shard_map(
        functools.partial(on_device, mesh.shape["img"], mesh.shape["txt"]),
        mesh=mesh,
        in_specs=(
            P(("img", "txt"), None),
            P(("txt", "img"), None),
            P(("txt", "img")),
            P(("txt", "img")),
        )
        + (P(),) * 10,
        out_specs=(P(("img", "txt"), None), P(("txt", "img"), None), P()),
        check_vma=False,
    )
```

```python
import functools

import jax
import jax.numpy as jnp
from jax import lax
from jax.experimental import pallas as pl
from jax.experimental.pallas import tpu as pltpu
from jax.sharding import PartitionSpec as P

HD = 256
EPSILON = 1e-05
MASKED = -1e30
FLOOR = -1e29
WINDOW = 8
COUNT_BASE = 4096
TILE = 16
MESH = pl.DeviceIdType.MESH
F32 = jnp.float32
BF16 = jnp.bfloat16


def normalize(tokens_in, gain_row):
    values = tokens_in.astype(F32)
    average = jnp.mean(values, axis=-1, keepdims=True)
    centered = values - average
    variance = jnp.mean(centered * centered, axis=-1, keepdims=True)
    return centered * lax.rsqrt(variance + EPSILON) * gain_row


def iota(shape, dim):
    return lax.broadcasted_iota(jnp.int32, shape, dim)


def fold(block):
    extra = block[TILE:]
    half = block.shape[1] // 2
    return jnp.concatenate([block[:TILE], jnp.concatenate([extra[:, :half], extra[:, half:]], axis=0)], axis=1)


def mm(a, b):
    return jnp.dot(a, b, preferred_element_type=F32)


def mm_t(a, b):
    return lax.dot_general(a, b, (((1,), (1,)), ((), ())), preferred_element_type=F32)


def kernel(
    n_img, n_txt,
    img_hbm, prompt_hbm, ids_hbm, valid_hbm, igain_hbm, pgain_hbm,
    wq_hbm, wk_hbm, wvi_hbm, wvp_hbm, woi_hbm, wop_hbm, iscale_hbm, pscale_hbm,
    out_img, out_prompt, out_cat,
    img_ref, prompt_ref, ids_ref, valid_ref, igain_ref, pgain_ref, iscale_ref, pscale_ref,
    wq, wk, wvi, wvp, woi, wop, xi, xp, meta, queries, keys, values_i, values_p, exp_c, exp_r, x_prompt,
    stat_r, stat_c, di_out, di_in, dp_out, dp_in, win, tally, cat,
    in_sem, w_sem, xi_s, xi_r, relay_s, xp_s, xp_r, meta_s, meta_r, sr_s, sr_r, sc_s, sc_r,
    di_s, di_r, dp_s, dp_r, win_s, win_r, tally_s, tally_r, cat_s, cat_r,
):
    my_img, my_txt = lax.axis_index("img"), lax.axis_index("txt")
    rows, width = img_ref.shape
    half = width // 2
    tokens = prompt_ref.shape[0]
    spare = tokens - TILE
    embed = wq.shape[1]
    heads = embed // HD
    n_rows = n_txt * rows
    n_cols = n_img * tokens
    cats = out_cat.shape[0]
    cat_lanes = tally.shape[2]

    inputs = (
        (prompt_hbm, prompt_ref), (pgain_hbm, pgain_ref), (valid_hbm, valid_ref), (ids_hbm, ids_ref),
        (img_hbm, img_ref), (igain_hbm, igain_ref), (iscale_hbm, iscale_ref), (pscale_hbm, pscale_ref),
    )
    fetches = [pltpu.make_async_copy(src, dst, in_sem.at[n]) for n, (src, dst) in enumerate(inputs)]
    weights = ((wq_hbm, wq), (wvi_hbm, wvi), (wk_hbm, wk), (wvp_hbm, wvp), (wop_hbm, wop), (woi_hbm, woi))
    loads = [pltpu.make_async_copy(src, dst, w_sem.at[n]) for n, (src, dst) in enumerate(weights)]
    for fetch in fetches:
        fetch.start()

    def others(axis, body):
        count, mine = (n_img, my_img) if axis == "img" else (n_txt, my_txt)
        if count <= 8:
            for step in sorted(range(1, count), key=lambda n: abs(2 * n - count)):
                body(lax.rem(mine + step, count))
        else:

            @pl.loop(1, count)
            def _(step):
                body(lax.rem(mine + step, count))

    def place(axis, p):
        return {"img": p, "txt": my_txt} if axis == "img" else {"img": my_img, "txt": p}

    barrier = pltpu.get_barrier_semaphore()
    for axis in ("img", "txt"):
        others(axis, lambda p: pl.semaphore_signal(barrier, inc=1, device_id=place(axis, p), device_id_type=MESH))
    for load in loads:
        load.start()

    def send(axis, src, dst, s, r):
        mine = my_img if axis == "img" else my_txt
        others(
            axis,
            lambda p: pltpu.make_async_remote_copy(
                src(p), dst.at[mine], s.at[0], r.at[0], device_id=place(axis, p), device_id_type=MESH
            ).start(),
        )

    def whole(buf, s, r):
        part = buf.at[pl.ds(0, buf.shape[0] - 1)]
        return pltpu.make_async_remote_copy(
            part, part, s.at[0], r.at[0], device_id={"img": my_img, "txt": my_txt}, device_id_type=MESH
        )

    for fetch in fetches[:4]:
        fetch.wait()
    xp[my_img] = fold(normalize(prompt_ref[...], pgain_ref[...].reshape(1, width))).astype(BF16)

    valid_row = valid_ref[...].reshape(1, tokens)
    ids_row = ids_ref[...].reshape(1, tokens)
    first_id = ids_row[:, 0:1]
    members = jnp.logical_and(ids_row - first_id == iota((WINDOW, tokens), 0), valid_row > 0).astype(F32)
    counts = jnp.sum(members, axis=1, keepdims=True).astype(jnp.int32)
    lane = iota((WINDOW, 128), 1) - (my_img % 8) * TILE
    slot = iota((WINDOW, 128), 0)
    own_lane = jnp.logical_and(jnp.logical_and(lane >= 0, lane < TILE), lane % WINDOW == slot)
    numbers = jnp.sum(jnp.where(own_lane, counts * COUNT_BASE + first_id + slot, 0), axis=0, keepdims=True)
    diagonal = iota((tokens, tokens), 0) == iota((tokens, tokens), 1)
    valid_col = jnp.sum(jnp.where(diagonal, jnp.broadcast_to(valid_row, (tokens, tokens)), 0), axis=1, keepdims=True)

    def marks(at, first, count):
        here = at + iota((count, 128), 0) == iota((count, 128), 1)
        return jnp.sum(jnp.where(here, valid_col[first : first + count], 0), axis=0, keepdims=True)

    meta[my_img] = jnp.concatenate(
        [numbers, marks((my_img % 8) * TILE, 0, TILE), marks((my_img % (128 // spare)) * spare, TILE, spare)], axis=1
    )

    fetches[4].wait()
    fetches[5].wait()
    xi[my_txt] = normalize(img_ref[...], igain_ref[...].reshape(1, width)).astype(BF16)

    pl.semaphore_wait(barrier, n_img - 1 + n_txt - 1)

    def image_copy(p, at):
        return pltpu.make_async_remote_copy(
            xi.at[at], xi.at[at], xi_s.at[p], xi_r.at[at], device_id=place("txt", p), device_id_type=MESH
        )

    mate = my_txt + 1 - 2 * (my_txt % 2)
    far = [lax.rem(my_txt + 2 * step, n_txt) for step in range(1, n_txt // 2)]
    send("img", lambda p: xp.at[my_img], xp, xp_s, xp_r)
    for p in far:
        image_copy(p, my_txt).start()
    image_copy(mate, my_txt).start()
    send("img", lambda p: meta.at[my_img], meta, meta_s, meta_r)

    def relay(p):
        return pltpu.make_async_remote_copy(
            xi.at[p], xi.at[p], relay_s.at[p], xi_r.at[p], device_id=place("txt", mate), device_id_type=MESH
        )

    for p in far:
        image_copy(p, p).wait_recv()
        relay(p).start()
    for load in loads[:4]:
        load.wait()

    def lanes(h):
        return pl.ds(pl.multiple_of(h * HD, HD), HD)

    whole(xp, xp_s, xp_r).wait_recv()
    tall = xp[:, :, :width].reshape(n_img * TILE, width)
    short = xp[:, :, width:].astype(F32)
    short = jnp.concatenate([short[:, :spare], short[:, spare:]], axis=2).reshape(n_img * spare, width)
    x_prompt[...] = jnp.concatenate([tall, short.astype(BF16)], axis=0)

    @pl.loop(0, heads)
    def _(h):
        keys[:, lanes(h)] = mm(x_prompt[...], wk[:, lanes(h)]).astype(BF16)
        values_p[:, lanes(h)] = mm(x_prompt[...], wvp[:, lanes(h)]).astype(BF16)

    image_copy(mate, mate).wait_recv()
    for p in far:
        beyond = p + 1 - 2 * (p % 2)
        image_copy(beyond, beyond).wait_recv()

    @pl.loop(0, heads)
    def _(h):
        x_image = xi[...].reshape(n_rows, width)
        queries[:, lanes(h)] = (mm(x_image, wq[:, lanes(h)]) * (HD ** -0.5)).astype(BF16)
        values_i[:, lanes(h)] = mm(x_image, wvi[:, lanes(h)]).astype(BF16)

    def over_heads(body, stats):
        if n_cols <= 512:
            for h in range(heads):
                stats = body(h, stats)
            return stats
        return lax.fori_loop(0, heads, body, stats)

    def head(h):
        return pl.ds(h * HD, HD) if isinstance(h, int) else pl.ds(pl.multiple_of(h * HD, HD), HD)

    def put(h, stats, top, total):
        at = iota(stats.shape, 1)
        return jnp.where(at == h, top, jnp.where(at == heads + h, total, stats))

    def column_head(h, stats):
        scores = mm_t(keys[:, head(h)], queries[:, head(h)])
        top = jnp.max(scores, axis=1, keepdims=True)
        exps = jnp.exp(scores - top)
        exp_c[h] = exps.astype(BF16)
        return put(h, stats, top, jnp.sum(exps, axis=1, keepdims=True))

    def row_head(h, stats):
        scores = jnp.where(mask, mm_t(queries[:, head(h)], keys[:, head(h)]), MASKED)
        top = jnp.maximum(jnp.max(scores, axis=1, keepdims=True), FLOOR)
        exps = jnp.exp(scores - top)
        exp_r[h] = exps.astype(BF16)
        return put(h, stats, top, jnp.sum(exps, axis=1, keepdims=True))

    stats = over_heads(column_head, jnp.zeros((n_cols, 128), F32))
    stat_c[my_img] = stats.T[: 2 * heads]
    send("img", lambda p: stat_c.at[my_img], stat_c, sc_s, sc_r)
    def factor(buf, mine):
        tops, sums = buf[:, :heads, :], buf[:, heads:, :]
        top = jnp.max(tops, axis=0)
        total = jnp.sum(sums * jnp.exp(tops - top[None]), axis=0)
        own = jnp.exp(buf[mine][:heads] - top) / total
        return jnp.concatenate([own, jnp.zeros((128 - heads, own.shape[1]), F32)], axis=0).T

    def numerators(exps, values):
        return [mm(exps[h], values[:, head(h)]) for h in range(heads)]

    def update(numers, scale, out_weight):
        delta = 0.0
        for h in range(heads):
            delta += mm((numers[h] * scale[:, h : h + 1]).astype(BF16), out_weight[head(h), :])
        return delta

    numers_p = numerators(exp_c, values_i)
    whole(meta, meta_s, meta_r).wait_recv()
    per = 128 // spare
    tall_marks = [jnp.sum(meta[g * 8 : g * 8 + 8, :, 128:256], axis=0) for g in range(n_img // 8)]
    short_marks = [jnp.sum(meta[g : min(g + per, n_img), :, 256:], axis=0) for g in range(0, n_img, per)]
    mask = jnp.concatenate(tall_marks + short_marks, axis=1)[:, :n_cols] > 0
    loads[4].wait()
    whole(stat_c, sc_s, sc_r).wait_recv()
    delta = update(numers_p, factor(stat_c, my_img), wop)
    tall = delta[: n_img * TILE].reshape(n_img, TILE, width)
    short = delta[n_img * TILE :].reshape(n_img, spare, width)
    short = jnp.concatenate([short[:, :, :half], short[:, :, half:]], axis=1)
    dp_out[...] = jnp.concatenate([tall, short], axis=2).astype(BF16)
    dp_in[my_img] = dp_out[my_img]
    send("img", lambda p: dp_out.at[p], dp_in, dp_s, dp_r)

    stats = over_heads(row_head, jnp.zeros((n_rows, 128), F32))
    stat_r[my_txt] = stats.T[: 2 * heads]
    send("txt", lambda p: stat_r.at[my_txt], stat_r, sr_s, sr_r)

    packed = jnp.concatenate([jnp.sum(meta[g * 8 : g * 8 + 8, :, :128], axis=0) for g in range(n_img // 8)], axis=1)
    key = jnp.broadcast_to(packed % COUNT_BASE, (cat_lanes, n_img * 16)) == iota((cat_lanes, n_img * 16), 0)
    low = iota((cat_lanes, n_img * 16), 1) % 16 < WINDOW
    pick_lo = jnp.where(jnp.logical_and(key, low), 1.0, 0.0).astype(BF16)
    pick_hi = jnp.where(jnp.logical_and(key, jnp.logical_not(low)), 1.0, 0.0).astype(BF16)
    numbers = jnp.broadcast_to((packed // COUNT_BASE).astype(F32), (8, n_img * 16)).astype(BF16)
    tally[my_txt] = mm_t(numbers, pick_lo)
    send("txt", lambda p: tally.at[my_txt], tally, tally_s, tally_r)

    numers_i = numerators(exp_r, values_p)

    whole(dp_in, dp_s, dp_r).wait_recv()
    total = jnp.sum(dp_in[...].astype(F32), axis=0)
    short = jnp.concatenate([total[:spare, width:], total[spare:, width:]], axis=1)
    prompt_delta = jnp.concatenate([total[:, :width], short], axis=0)
    fetches[6].wait()
    fetches[7].wait()
    joined = prompt_ref[...].astype(F32) + pscale_ref[...].reshape(1, width) * prompt_delta
    sums = jnp.dot(members, joined, precision=lax.Precision.HIGHEST, preferred_element_type=F32)
    win[my_img] = jnp.concatenate([sums[:, :half], sums[:, half:]], axis=0).astype(BF16)
    send("img", lambda p: win.at[my_img], win, win_s, win_r)
    out_prompt[...] = joined.astype(BF16)

    loads[5].wait()
    whole(stat_r, sr_s, sr_r).wait_recv()
    di_out[...] = update(numers_i, factor(stat_r, my_txt), woi).astype(BF16).reshape(di_out.shape)
    di_in[my_txt] = di_out[my_txt]
    send("txt", lambda p: di_out.at[p], di_in, di_s, di_r)

    whole(win, win_s, win_r).wait_recv()
    windows = win[...].reshape(n_img * 16, half)
    block = jnp.concatenate([mm(pick_lo[:cats], windows), mm(pick_hi[:cats], windows)], axis=1)
    cat[my_txt] = block.astype(BF16)
    send("txt", lambda p: cat.at[my_txt], cat, cat_s, cat_r)

    whole(di_in, di_s, di_r).wait_recv()
    image_delta = jnp.sum(di_in[...].astype(F32), axis=0)
    out_img[...] = (img_ref[...].astype(F32) + iscale_ref[...].reshape(1, width) * image_delta).astype(BF16)

    whole(tally, tally_s, tally_r).wait_recv()
    tally_row = jnp.sum(tally[...], axis=0)[0:1]
    on_diagonal = iota((cats, cat_lanes), 0) == iota((cats, cat_lanes), 1)
    tally_col = jnp.sum(jnp.where(on_diagonal, tally_row, 0.0), axis=1, keepdims=True)
    whole(cat, cat_s, cat_r).wait_recv()
    out_cat[...] = jnp.sum(cat[...].astype(F32), axis=0) / tally_col

    for p in far:
        image_copy(p, my_txt).wait_send()
        relay(p).wait_send()
    image_copy(mate, my_txt).wait_send()
    for buf, s, r in (
        (xp, xp_s, xp_r), (meta, meta_s, meta_r), (stat_c, sc_s, sc_r), (stat_r, sr_s, sr_r), (dp_in, dp_s, dp_r),
        (tally, tally_s, tally_r), (di_in, di_s, di_r), (win, win_s, win_r), (cat, cat_s, cat_r),
    ):
        whole(buf, s, r).wait_send()


def keep(*refs):
    count = len(refs) // 2
    for n in range(count):
        refs[count + n][...] = refs[n][...]


def on_device(n_img, n_txt, image_tokens, prompt_tokens, *rest):
    rows, width = image_tokens.shape
    tokens = prompt_tokens.shape[0]
    embed = rest[4].shape[1]
    heads = embed // HD
    n_rows, n_cols = n_txt * rows, n_img * tokens
    folded = width + width // 2
    cats = n_img * n_txt * tokens // 16
    cat_lanes = (cats + 127) // 128 * 128
    vmem, hbm = pl.BlockSpec(memory_space=pltpu.VMEM), pl.BlockSpec(memory_space=pl.ANY)
    dma = pltpu.SemaphoreType.DMA
    one = (dma((1,)), dma((1,)))
    outs = (
        jax.ShapeDtypeStruct((rows, width), BF16),
        jax.ShapeDtypeStruct((tokens, width), BF16),
        jax.ShapeDtypeStruct((cats, width), F32),
    )
    results = pl.pallas_call(
        functools.partial(kernel, n_img, n_txt),
        out_shape=tuple(pltpu.VMEM(out.shape, out.dtype) for out in outs),
        in_specs=[hbm] * 14,
        out_specs=(vmem, vmem, vmem),
        scratch_shapes=[pltpu.VMEM(x.shape, x.dtype) for x in (image_tokens, prompt_tokens, *rest[:4], *rest[10:])]
        + [pltpu.VMEM((width, embed), BF16)] * 4
        + [pltpu.VMEM((embed, width), BF16)] * 2
        + [
            pltpu.VMEM((n_txt, rows, width), BF16),
            pltpu.VMEM((n_img, TILE, folded), BF16),
            pltpu.VMEM((n_img, 1, 384), jnp.int32),
            pltpu.VMEM((n_rows, embed), BF16),
            pltpu.VMEM((n_cols, embed), BF16),
            pltpu.VMEM((n_rows, embed), BF16),
            pltpu.VMEM((n_cols, embed), BF16),
            pltpu.VMEM((heads, n_cols, n_rows), BF16),
            pltpu.VMEM((heads, n_rows, n_cols), BF16),
            pltpu.VMEM((n_cols, width), BF16),
            pltpu.VMEM((n_txt, 2 * heads, n_rows), F32),
            pltpu.VMEM((n_img, 2 * heads, n_cols), F32),
            pltpu.VMEM((n_txt, rows, width), BF16),
            pltpu.VMEM((n_txt, rows, width), BF16),
            pltpu.VMEM((n_img, TILE, folded), BF16),
            pltpu.VMEM((n_img, TILE, folded), BF16),
            pltpu.VMEM((n_img, 16, width // 2), BF16),
            pltpu.VMEM((n_txt, 8, cat_lanes), F32),
            pltpu.VMEM((n_txt, cats, width), BF16),
            dma((8,)),
            dma((6,)),
            dma((n_txt,)),
            dma((n_txt,)),
            dma((n_txt,)),
            *one, *one, *one, *one, *one, *one, *one, *one, *one,
        ],
        compiler_params=pltpu.CompilerParams(
            collective_id=0, has_side_effects=True, vmem_limit_bytes=56 * 2**20
        ),
        name="joining_layer",
    )(image_tokens, prompt_tokens, *rest)
    return pl.pallas_call(
        keep,
        out_shape=outs,
        in_specs=[vmem] * len(outs),
        out_specs=(vmem,) * len(outs),
        compiler_params=pltpu.CompilerParams(vmem_limit_bytes=2**20),
        name="keep",
    )(*results)


def solution(mesh):
    return jax.shard_map(
        functools.partial(on_device, mesh.shape["img"], mesh.shape["txt"]),
        mesh=mesh,
        in_specs=(
            P(("img", "txt"), None),
            P(("txt", "img"), None),
            P(("txt", "img")),
            P(("txt", "img")),
        )
        + (P(),) * 10,
        out_specs=(P(("img", "txt"), None), P(("txt", "img"), None), P()),
        check_vma=False,
    )
```

```python
import functools

import jax
import jax.numpy as jnp
from jax import lax
from jax.experimental import pallas as pl
from jax.experimental.pallas import tpu as pltpu
from jax.sharding import PartitionSpec as P

HD = 256
EPSILON = 1e-05
MASKED = -1e30
FLOOR = -1e29
WINDOW = 8
COUNT_BASE = 4096
TILE = 16
MESH = pl.DeviceIdType.MESH
F32 = jnp.float32
BF16 = jnp.bfloat16


def normalize(tokens_in, gain_row):
    values = tokens_in.astype(F32)
    average = jnp.mean(values, axis=-1, keepdims=True)
    centered = values - average
    variance = jnp.mean(centered * centered, axis=-1, keepdims=True)
    return centered * lax.rsqrt(variance + EPSILON) * gain_row


def iota(shape, dim):
    return lax.broadcasted_iota(jnp.int32, shape, dim)


def fold(block):
    extra = block[TILE:]
    half = block.shape[1] // 2
    return jnp.concatenate([block[:TILE], jnp.concatenate([extra[:, :half], extra[:, half:]], axis=0)], axis=1)


def mm(a, b):
    return jnp.dot(a, b, preferred_element_type=F32)


def mm_t(a, b):
    return lax.dot_general(a, b, (((1,), (1,)), ((), ())), preferred_element_type=F32)


def kernel(
    n_img, n_txt,
    img_hbm, prompt_hbm, ids_hbm, valid_hbm, igain_hbm, pgain_hbm,
    wq_hbm, wk_hbm, wvi_hbm, wvp_hbm, woi_hbm, wop_hbm, iscale_hbm, pscale_hbm,
    out_img, out_prompt, out_cat,
    img_ref, prompt_ref, ids_ref, valid_ref, igain_ref, pgain_ref, iscale_ref, pscale_ref,
    wq, wk, wvi, wvp, woi, wop, xi, xp, meta, queries, keys, values_i, values_p, exp_c, exp_r,
    stat_r, stat_c, di_out, di_in, dp_out, dp_in, win, tally, cat,
    in_sem, w_sem, xi_s, xi_r, relay_s, xp_s, xp_r, meta_s, meta_r, sr_s, sr_r, sc_s, sc_r,
    di_s, di_r, dp_s, dp_r, win_s, win_r, tally_s, tally_r, cat_s, cat_r,
):
    my_img, my_txt = lax.axis_index("img"), lax.axis_index("txt")
    rows, width = img_ref.shape
    half = width // 2
    tokens = prompt_ref.shape[0]
    spare = tokens - TILE
    embed = wq.shape[1]
    heads = embed // HD
    n_rows = n_txt * rows
    n_cols = n_img * tokens
    cats = out_cat.shape[0]
    cat_lanes = tally.shape[2]

    inputs = (
        (prompt_hbm, prompt_ref), (pgain_hbm, pgain_ref), (valid_hbm, valid_ref), (ids_hbm, ids_ref),
        (img_hbm, img_ref), (igain_hbm, igain_ref), (iscale_hbm, iscale_ref), (pscale_hbm, pscale_ref),
    )
    fetches = [pltpu.make_async_copy(src, dst, in_sem.at[n]) for n, (src, dst) in enumerate(inputs)]
    weights = ((wq_hbm, wq), (wvi_hbm, wvi), (wk_hbm, wk), (wvp_hbm, wvp), (wop_hbm, wop), (woi_hbm, woi))
    loads = [pltpu.make_async_copy(src, dst, w_sem.at[n]) for n, (src, dst) in enumerate(weights)]
    for fetch in fetches:
        fetch.start()

    def others(axis, body):
        count, mine = (n_img, my_img) if axis == "img" else (n_txt, my_txt)
        if count <= 8:
            for step in sorted(range(1, count), key=lambda n: abs(2 * n - count)):
                body(lax.rem(mine + step, count))
        else:

            @pl.loop(1, count)
            def _(step):
                body(lax.rem(mine + step, count))

    def place(axis, p):
        return {"img": p, "txt": my_txt} if axis == "img" else {"img": my_img, "txt": p}

    barrier = pltpu.get_barrier_semaphore()
    for axis in ("img", "txt"):
        others(axis, lambda p: pl.semaphore_signal(barrier, inc=1, device_id=place(axis, p), device_id_type=MESH))
    for load in loads:
        load.start()

    def send(axis, src, dst, s, r):
        mine = my_img if axis == "img" else my_txt
        others(
            axis,
            lambda p: pltpu.make_async_remote_copy(
                src(p), dst.at[mine], s.at[0], r.at[0], device_id=place(axis, p), device_id_type=MESH
            ).start(),
        )

    def whole(buf, s, r):
        part = buf.at[pl.ds(0, buf.shape[0] - 1)]
        return pltpu.make_async_remote_copy(
            part, part, s.at[0], r.at[0], device_id={"img": my_img, "txt": my_txt}, device_id_type=MESH
        )

    for fetch in fetches[:4]:
        fetch.wait()
    xp[my_img] = fold(normalize(prompt_ref[...], pgain_ref[...].reshape(1, width))).astype(BF16)

    valid_row = valid_ref[...].reshape(1, tokens)
    ids_row = ids_ref[...].reshape(1, tokens)
    first_id = ids_row[:, 0:1]
    members = jnp.logical_and(ids_row - first_id == iota((WINDOW, tokens), 0), valid_row > 0).astype(F32)
    counts = jnp.sum(members, axis=1, keepdims=True).astype(jnp.int32)
    lane = iota((WINDOW, 128), 1) - (my_img % 8) * TILE
    slot = iota((WINDOW, 128), 0)
    own_lane = jnp.logical_and(jnp.logical_and(lane >= 0, lane < TILE), lane % WINDOW == slot)
    numbers = jnp.sum(jnp.where(own_lane, counts * COUNT_BASE + first_id + slot, 0), axis=0, keepdims=True)
    diagonal = iota((tokens, tokens), 0) == iota((tokens, tokens), 1)
    valid_col = jnp.sum(jnp.where(diagonal, jnp.broadcast_to(valid_row, (tokens, tokens)), 0), axis=1, keepdims=True)

    def marks(at, first, count):
        here = at + iota((count, 128), 0) == iota((count, 128), 1)
        return jnp.sum(jnp.where(here, valid_col[first : first + count], 0), axis=0, keepdims=True)

    meta[my_img] = jnp.concatenate(
        [numbers, marks((my_img % 8) * TILE, 0, TILE), marks((my_img % (128 // spare)) * spare, TILE, spare)], axis=1
    )

    fetches[4].wait()
    fetches[5].wait()
    xi[my_txt] = normalize(img_ref[...], igain_ref[...].reshape(1, width)).astype(BF16)

    pl.semaphore_wait(barrier, n_img - 1 + n_txt - 1)

    def image_copy(p, at):
        return pltpu.make_async_remote_copy(
            xi.at[at], xi.at[at], xi_s.at[p], xi_r.at[at], device_id=place("txt", p), device_id_type=MESH
        )

    mate = my_txt + 1 - 2 * (my_txt % 2)
    far = [lax.rem(my_txt + 2 * step, n_txt) for step in range(1, n_txt // 2)]
    send("img", lambda p: xp.at[my_img], xp, xp_s, xp_r)
    for p in far:
        image_copy(p, my_txt).start()
    image_copy(mate, my_txt).start()
    send("img", lambda p: meta.at[my_img], meta, meta_s, meta_r)

    def image_rows(p):
        return pl.ds(pl.multiple_of(p * rows, rows), rows)

    def project_queries(p):
        queries[image_rows(p), :] = (mm(xi[p], wq[...]) * (HD ** -0.5)).astype(BF16)

    def project_values(p):
        values_i[image_rows(p), :] = mm(xi[p], wvi[...]).astype(BF16)

    def relay(p):
        return pltpu.make_async_remote_copy(
            xi.at[p], xi.at[p], relay_s.at[p], xi_r.at[p], device_id=place("txt", mate), device_id_type=MESH
        )

    loads[0].wait()
    project_queries(my_txt)
    for p in far:
        image_copy(p, p).wait_recv()
        relay(p).start()
    loads[1].wait()
    project_values(my_txt)
    image_copy(mate, mate).wait_recv()
    project_queries(mate)
    project_values(mate)
    for p in far:
        project_queries(p)
        project_values(p)

    whole(xp, xp_s, xp_r).wait_recv()
    tall = xp[:, :, :width].reshape(n_img * TILE, width)
    short = xp[:, :, width:].astype(F32)
    short = jnp.concatenate([short[:, :spare], short[:, spare:]], axis=2).reshape(n_img * spare, width)
    x_prompt = jnp.concatenate([tall, short.astype(BF16)], axis=0)
    loads[2].wait()
    keys[...] = mm(x_prompt, wk[...]).astype(BF16)
    beyond = [p + 1 - 2 * (p % 2) for p in far]
    for p in beyond:
        image_copy(p, p).wait_recv()
        project_queries(p)

    def over_heads(body, stats, first=0, last=heads):
        if n_cols <= 512:
            for h in range(first, last):
                stats = body(h, stats)
            return stats
        return lax.fori_loop(first, last, body, stats)

    def head(h):
        return pl.ds(h * HD, HD) if isinstance(h, int) else pl.ds(pl.multiple_of(h * HD, HD), HD)

    def put(h, stats, top, total):
        at = iota(stats.shape, 1)
        return jnp.where(at == h, top, jnp.where(at == heads + h, total, stats))

    def column_head(h, stats):
        scores = mm_t(keys[:, head(h)], queries[:, head(h)])
        top = jnp.max(scores, axis=1, keepdims=True)
        exps = jnp.exp(scores - top)
        exp_c[h] = exps.astype(BF16)
        return put(h, stats, top, jnp.sum(exps, axis=1, keepdims=True))

    def row_head(h, stats):
        scores = jnp.where(mask, mm_t(queries[:, head(h)], keys[:, head(h)]), MASKED)
        top = jnp.maximum(jnp.max(scores, axis=1, keepdims=True), FLOOR)
        exps = jnp.exp(scores - top)
        exp_r[h] = exps.astype(BF16)
        return put(h, stats, top, jnp.sum(exps, axis=1, keepdims=True))

    stats = over_heads(column_head, jnp.zeros((n_cols, 128), F32))
    stat_c[my_img] = stats.T[: 2 * heads]
    send("img", lambda p: stat_c.at[my_img], stat_c, sc_s, sc_r)
    def factor(buf, mine):
        tops, sums = buf[:, :heads, :], buf[:, heads:, :]
        top = jnp.max(tops, axis=0)
        total = jnp.sum(sums * jnp.exp(tops - top[None]), axis=0)
        own = jnp.exp(buf[mine][:heads] - top) / total
        return jnp.concatenate([own, jnp.zeros((128 - heads, own.shape[1]), F32)], axis=0).T

    def numerators(exps, values):
        return [mm(exps[h], values[:, head(h)]) for h in range(heads)]

    def update(numers, scale, out_weight):
        delta = 0.0
        for h in range(heads):
            delta += mm((numers[h] * scale[:, h : h + 1]).astype(BF16), out_weight[head(h), :])
        return delta

    for p in beyond:
        project_values(p)
    numers_p = numerators(exp_c, values_i)
    loads[3].wait()
    values_p[...] = mm(x_prompt, wvp[...]).astype(BF16)
    whole(meta, meta_s, meta_r).wait_recv()
    per = 128 // spare
    tall_marks = [jnp.sum(meta[g * 8 : g * 8 + 8, :, 128:256], axis=0) for g in range(n_img // 8)]
    short_marks = [jnp.sum(meta[g : min(g + per, n_img), :, 256:], axis=0) for g in range(0, n_img, per)]
    mask = jnp.concatenate(tall_marks + short_marks, axis=1)[:, :n_cols] > 0
    row_stats = over_heads(row_head, jnp.zeros((n_rows, 128), F32), 0, heads // 2)
    loads[4].wait()
    whole(stat_c, sc_s, sc_r).wait_recv()
    delta = update(numers_p, factor(stat_c, my_img), wop)
    tall = delta[: n_img * TILE].reshape(n_img, TILE, width)
    short = delta[n_img * TILE :].reshape(n_img, spare, width)
    short = jnp.concatenate([short[:, :, :half], short[:, :, half:]], axis=1)
    dp_out[...] = jnp.concatenate([tall, short], axis=2).astype(BF16)
    dp_in[my_img] = dp_out[my_img]
    send("img", lambda p: dp_out.at[p], dp_in, dp_s, dp_r)

    row_stats = over_heads(row_head, row_stats, heads // 2, heads)
    stat_r[my_txt] = row_stats.T[: 2 * heads]
    send("txt", lambda p: stat_r.at[my_txt], stat_r, sr_s, sr_r)

    packed = jnp.concatenate([jnp.sum(meta[g * 8 : g * 8 + 8, :, :128], axis=0) for g in range(n_img // 8)], axis=1)
    key = jnp.broadcast_to(packed % COUNT_BASE, (cat_lanes, n_img * 16)) == iota((cat_lanes, n_img * 16), 0)
    low = iota((cat_lanes, n_img * 16), 1) % 16 < WINDOW
    pick_lo = jnp.where(jnp.logical_and(key, low), 1.0, 0.0).astype(BF16)
    pick_hi = jnp.where(jnp.logical_and(key, jnp.logical_not(low)), 1.0, 0.0).astype(BF16)
    numbers = jnp.broadcast_to((packed // COUNT_BASE).astype(F32), (8, n_img * 16)).astype(BF16)
    tally[my_txt] = mm_t(numbers, pick_lo)
    send("txt", lambda p: tally.at[my_txt], tally, tally_s, tally_r)

    whole(dp_in, dp_s, dp_r).wait_recv()
    total = jnp.sum(dp_in[...].astype(F32), axis=0)
    short = jnp.concatenate([total[:spare, width:], total[spare:, width:]], axis=1)
    prompt_delta = jnp.concatenate([total[:, :width], short], axis=0)
    fetches[6].wait()
    fetches[7].wait()
    joined = prompt_ref[...].astype(F32) + pscale_ref[...].reshape(1, width) * prompt_delta
    sums = jnp.dot(members, joined, precision=lax.Precision.HIGHEST, preferred_element_type=F32)
    win[my_img] = jnp.concatenate([sums[:, :half], sums[:, half:]], axis=0).astype(BF16)
    send("img", lambda p: win.at[my_img], win, win_s, win_r)
    out_prompt[...] = joined.astype(BF16)

    numers_i = numerators(exp_r, values_p)
    loads[5].wait()
    whole(stat_r, sr_s, sr_r).wait_recv()
    di_out[...] = update(numers_i, factor(stat_r, my_txt), woi).astype(BF16).reshape(di_out.shape)
    di_in[my_txt] = di_out[my_txt]
    send("txt", lambda p: di_out.at[p], di_in, di_s, di_r)

    whole(win, win_s, win_r).wait_recv()
    windows = win[...].reshape(n_img * 16, half)
    block = jnp.concatenate([mm(pick_lo[:cats], windows), mm(pick_hi[:cats], windows)], axis=1)
    cat[my_txt] = block.astype(BF16)
    send("txt", lambda p: cat.at[my_txt], cat, cat_s, cat_r)

    whole(di_in, di_s, di_r).wait_recv()
    image_delta = jnp.sum(di_in[...].astype(F32), axis=0)
    out_img[...] = (img_ref[...].astype(F32) + iscale_ref[...].reshape(1, width) * image_delta).astype(BF16)

    whole(tally, tally_s, tally_r).wait_recv()
    tally_row = jnp.sum(tally[...], axis=0)[0:1]
    on_diagonal = iota((cats, cat_lanes), 0) == iota((cats, cat_lanes), 1)
    tally_col = jnp.sum(jnp.where(on_diagonal, tally_row, 0.0), axis=1, keepdims=True)
    whole(cat, cat_s, cat_r).wait_recv()
    out_cat[...] = jnp.sum(cat[...].astype(F32), axis=0) / tally_col

    for p in far:
        image_copy(p, my_txt).wait_send()
        relay(p).wait_send()
    image_copy(mate, my_txt).wait_send()
    for buf, s, r in (
        (xp, xp_s, xp_r), (meta, meta_s, meta_r), (stat_c, sc_s, sc_r), (stat_r, sr_s, sr_r), (dp_in, dp_s, dp_r),
        (tally, tally_s, tally_r), (di_in, di_s, di_r), (win, win_s, win_r), (cat, cat_s, cat_r),
    ):
        whole(buf, s, r).wait_send()


def keep(*refs):
    count = len(refs) // 2
    for n in range(count):
        refs[count + n][...] = refs[n][...]


def on_device(n_img, n_txt, image_tokens, prompt_tokens, *rest):
    rows, width = image_tokens.shape
    tokens = prompt_tokens.shape[0]
    embed = rest[4].shape[1]
    heads = embed // HD
    n_rows, n_cols = n_txt * rows, n_img * tokens
    folded = width + width // 2
    cats = n_img * n_txt * tokens // 16
    cat_lanes = (cats + 127) // 128 * 128
    vmem, hbm = pl.BlockSpec(memory_space=pltpu.VMEM), pl.BlockSpec(memory_space=pl.ANY)
    dma = pltpu.SemaphoreType.DMA
    one = (dma((1,)), dma((1,)))
    outs = (
        jax.ShapeDtypeStruct((rows, width), BF16),
        jax.ShapeDtypeStruct((tokens, width), BF16),
        jax.ShapeDtypeStruct((cats, width), F32),
    )
    results = pl.pallas_call(
        functools.partial(kernel, n_img, n_txt),
        out_shape=tuple(pltpu.VMEM(out.shape, out.dtype) for out in outs),
        in_specs=[hbm] * 14,
        out_specs=(vmem, vmem, vmem),
        scratch_shapes=[pltpu.VMEM(x.shape, x.dtype) for x in (image_tokens, prompt_tokens, *rest[:4], *rest[10:])]
        + [pltpu.VMEM((width, embed), BF16)] * 4
        + [pltpu.VMEM((embed, width), BF16)] * 2
        + [
            pltpu.VMEM((n_txt, rows, width), BF16),
            pltpu.VMEM((n_img, TILE, folded), BF16),
            pltpu.VMEM((n_img, 1, 384), jnp.int32),
            pltpu.VMEM((n_rows, embed), BF16),
            pltpu.VMEM((n_cols, embed), BF16),
            pltpu.VMEM((n_rows, embed), BF16),
            pltpu.VMEM((n_cols, embed), BF16),
            pltpu.VMEM((heads, n_cols, n_rows), BF16),
            pltpu.VMEM((heads, n_rows, n_cols), BF16),
            pltpu.VMEM((n_txt, 2 * heads, n_rows), F32),
            pltpu.VMEM((n_img, 2 * heads, n_cols), F32),
            pltpu.VMEM((n_txt, rows, width), BF16),
            pltpu.VMEM((n_txt, rows, width), BF16),
            pltpu.VMEM((n_img, TILE, folded), BF16),
            pltpu.VMEM((n_img, TILE, folded), BF16),
            pltpu.VMEM((n_img, 16, width // 2), BF16),
            pltpu.VMEM((n_txt, 8, cat_lanes), F32),
            pltpu.VMEM((n_txt, cats, width), BF16),
            dma((8,)),
            dma((6,)),
            dma((n_txt,)),
            dma((n_txt,)),
            dma((n_txt,)),
            *one, *one, *one, *one, *one, *one, *one, *one, *one,
        ],
        compiler_params=pltpu.CompilerParams(
            collective_id=0, has_side_effects=True, vmem_limit_bytes=56 * 2**20
        ),
        name="joining_layer",
    )(image_tokens, prompt_tokens, *rest)
    return pl.pallas_call(
        keep,
        out_shape=outs,
        in_specs=[vmem] * len(outs),
        out_specs=(vmem,) * len(outs),
        compiler_params=pltpu.CompilerParams(vmem_limit_bytes=2**20),
        name="keep",
    )(*results)


def solution(mesh):
    return jax.shard_map(
        functools.partial(on_device, mesh.shape["img"], mesh.shape["txt"]),
        mesh=mesh,
        in_specs=(
            P(("img", "txt"), None),
            P(("txt", "img"), None),
            P(("txt", "img")),
            P(("txt", "img")),
        )
        + (P(),) * 10,
        out_specs=(P(("img", "txt"), None), P(("txt", "img"), None), P()),
        check_vma=False,
    )
```
